512 devices in a mesh: wide: 32 (over x, z_hi, core), narrow: 16 (over z_lo, y).
Axes of the slice: x: 4, y: 4, z: 16 (z_hi: 4, z_lo: 4; z = z_hi * 4 + z_lo), core: 2. Of those that a mesh axis runs over, the one named last changes fastest.
Arguments:
- source: float32 [512, 512, 128], P(('wide', 'narrow')), may hold values from -6 to 6
- pressure_start: float32 [512, 512, 128], P(('wide', 'narrow')), may hold values from -6 to 6
- trans_x: float32 [512, 512, 128], P(('wide', 'narrow')), may hold values from 0.1 to 10
- trans_y: float32 [512, 512, 128], P(('wide', 'narrow')), may hold values from 0.1 to 10
- trans_z: float32 [512, 512, 128], P(('wide', 'narrow')), may hold values from 0.1 to 4
- storage: float32 [512, 512, 128], P(('wide', 'narrow')), may hold values from 0.2 to 2
- adjoint_seed: float32 [512, 512, 128], P(('wide', 'narrow')), may hold values from -6 to 6
- comp_cell: int32 [512, 64], P(('wide', 'narrow')), may hold values from 0 to 65535
- comp_well: int32 [512, 64], P(('wide', 'narrow')), may hold values from 0 to 20479
- comp_count: int32 [512], P(('wide', 'narrow')), may hold values from 1 to 64, as said below
- well_slot: int32 [20480], replicated, may hold values from 0 to 20479, each once
Outputs:
- grad_source: float32 [512, 512, 128], P(('wide', 'narrow'))
- well_sens: float32 [20480], P(('wide', 'narrow'))
The draws below stay inside these ranges and needn't reach their ends.
Inputs may be any that keep to these rules, and one draw needn't show every extreme that they name: `comp_count`: every row has at least one live slot, and some row has all 64 live.
All inputs are finite; a program needn't handle non-finite values.
Results may differ from the reference program's by a relative error of at most 0.0003.
Values sent between devices are 32-bit elements; how exact they have to be, the bound alone decides.
A program may use at most 128 MiB of HBM per device.

```python
import math
import jax
import jax.numpy as jnp
from jax import lax

K = 128
ITERS = 2
CAP = 64
NX = 512
NY = 512
WELLS = 20480


def draw_comp_count(key, part):
    key = jax.random.fold_in(key, 7)
    first_key, second_key = jax.random.split(key)
    shifts = jax.random.randint(first_key, (NY,), 0, 6)
    chosen = jax.random.randint(second_key, (), 0, NY)
    shifts = shifts.at[chosen].set(0)
    counts = jnp.right_shift(jnp.full((NY,), CAP, jnp.int32), shifts.astype(jnp.int32))
    return jnp.maximum(counts, 1).astype(jnp.int32)


def touch_ends(values, own_key, smallest, top_value):
    longest = values.shape.index(max(values.shape))
    spots = []
    for shift in (0, 1):
        where = [jax.random.randint(jax.random.fold_in(own_key, axis), (), 0, length) for axis, length in enumerate(values.shape)]
        where[longest] = (where[longest] + shift) % values.shape[longest]
        spots.append(tuple(where))
    return values.at[spots[0]].set(smallest).at[spots[1]].set(top_value)


def levels(rng, shape, pieces, smallest, high):
    gain, own = 1.0, jax.random.fold_in(rng, 6)
    for position, shards_of in pieces:
        draws = jnp.exp(jax.random.uniform(jax.random.fold_in(own, position), (shards_of,), jnp.float32, smallest / len(pieces), high / len(pieces)))
        gain = gain * jnp.repeat(draws, shape[position] // shards_of).reshape([-1 if axis == position else 1 for axis in range(len(shape))])
    return gain


def scatter_about(key, shape, deviation, reach, pieces=(), held_as=jnp.bfloat16):
    level = levels(key, shape, pieces, -0.22, 0.18) if pieces else 1.0
    result = jax.random.normal(key, shape, jnp.float32) * deviation * level
    return jnp.minimum(jnp.maximum(result, -reach), reach).astype(held_as)


def setup_inputs(seed: int = 0) -> dict:
    key_of = jax.random.split(jax.random.key(seed), 12)
    return {
        "source": scatter_about(key_of[0], (NY, NX, K), 1.0, 6.0, ((0, 512),), jnp.float32),
        "pressure_start": scatter_about(key_of[1], (NY, NX, K), 1.0, 6.0, ((0, 512),), jnp.float32),
        "trans_x": jnp.clip(jnp.exp(math.log(10.0) - 4.6051702 * jax.random.uniform(key_of[2], (NY, NX, K), jnp.float32) ** levels(key_of[2], (NY, NX, K), ((0, 512),), -0.2, 0.2)), 0.1, 10.0),
        "trans_y": jnp.clip(jnp.exp(math.log(10.0) - 4.6051702 * jax.random.uniform(key_of[3], (NY, NX, K), jnp.float32) ** levels(key_of[3], (NY, NX, K), ((0, 512),), -0.2, 0.2)), 0.1, 10.0),
        "trans_z": jnp.clip(jnp.exp(math.log(4.0) - 3.6888794 * jax.random.uniform(key_of[4], (NY, NX, K), jnp.float32) ** levels(key_of[4], (NY, NX, K), ((0, 512),), -0.2, 0.2)), 0.1, 4.0),
        "storage": jnp.clip(jnp.exp(math.log(2.0) - 2.3025851 * jax.random.uniform(key_of[5], (NY, NX, K), jnp.float32) ** levels(key_of[5], (NY, NX, K), ((0, 512),), -0.2, 0.2)), 0.2, 2.0),
        "adjoint_seed": scatter_about(key_of[6], (NY, NX, K), 1.0, 6.0, ((0, 512),), jnp.float32),
        "comp_cell": touch_ends(jax.random.randint(key_of[7], (NY, CAP), 0, NX * K), jax.random.fold_in(key_of[7], 1), 0, (NX * K) - 1).astype(jnp.int32),
        "comp_well": touch_ends(jax.random.randint(key_of[8], (NY, CAP), 0, WELLS), jax.random.fold_in(key_of[8], 1), 0, WELLS - 1).astype(jnp.int32),
        "comp_count": draw_comp_count(jax.random.fold_in(key_of[11], 71), 0),
        "well_slot": jax.random.permutation(key_of[10], WELLS).astype(jnp.int32),
    }


def shifted(values, offset, axis_dim):
    extent = values.shape[axis_dim]
    if offset > 0:
        kept = lax.slice_in_dim(values, 0, extent - offset, axis=axis_dim)
        zero_part = jnp.zeros_like(lax.slice_in_dim(values, 0, offset, axis=axis_dim))
        return jnp.concatenate([zero_part, kept], axis=axis_dim)
    kept = lax.slice_in_dim(values, -offset, extent, axis=axis_dim)
    zero_part = jnp.zeros_like(lax.slice_in_dim(values, 0, -offset, axis=axis_dim))
    return jnp.concatenate([kept, zero_part], axis=axis_dim)


def factor_lines(trans, storage, axis_dim):
    extent = trans.shape[axis_dim]
    lower_band = -shifted(trans, 1, axis_dim)
    upper_band = -trans
    middle = storage + trans + shifted(trans, 1, axis_dim)
    factors = []
    stride = 1
    while stride < extent:
        below_mid = shifted(middle - 1.0, stride, axis_dim) + 1.0
        above_mid = shifted(middle - 1.0, -stride, axis_dim) + 1.0
        left_gain = lower_band / below_mid
        right_gain = upper_band / above_mid
        new_lower = -left_gain * shifted(lower_band, stride, axis_dim)
        new_upper = -right_gain * shifted(upper_band, -stride, axis_dim)
        middle = middle - left_gain * shifted(upper_band, stride, axis_dim) - right_gain * shifted(lower_band, -stride, axis_dim)
        lower_band, upper_band = new_lower, new_upper
        factors.append((stride, left_gain, right_gain))
        stride = stride * 2
    return factors, middle


def solve_lines(factored, right_side, axis_dim):
    factors, middle = factored
    for stride, left_gain, right_gain in factors:
        right_side = right_side - left_gain * shifted(right_side, stride, axis_dim) - right_gain * shifted(right_side, -stride, axis_dim)
    return right_side / middle


def divergence(values, trans, axis_dim):
    face_flux = trans * (values - shifted(values, -1, axis_dim))
    return face_flux - shifted(face_flux, 1, axis_dim)


def face_product(first_field, second_field, axis_dim):
    return (first_field - shifted(first_field, -1, axis_dim)) * (second_field - shifted(second_field, -1, axis_dim))


def face_to_cells(face_sens, axis_dim):
    return 0.5 * (face_sens + shifted(face_sens, 1, axis_dim))


def reference(source, pressure_start, trans_x, trans_y, trans_z, storage, adjoint_seed, comp_cell, comp_well, comp_count, well_slot):
    full_shape = source.shape
    open_x = jnp.where(lax.broadcasted_iota(jnp.int32, full_shape, 1) < full_shape[1] - 1, trans_x, 0.0)
    open_y = jnp.where(lax.broadcasted_iota(jnp.int32, full_shape, 0) < full_shape[0] - 1, trans_y, 0.0)
    open_z = jnp.where(lax.broadcasted_iota(jnp.int32, full_shape, 2) < full_shape[2] - 1, trans_z, 0.0)
    factor_x = factor_lines(open_x, storage, 1)
    factor_y = factor_lines(open_y, storage, 0)
    pressure = pressure_start
    states = []
    for iteration in range(ITERS):
        middle_field = solve_lines(factor_x, source - divergence(pressure, open_y, 0) - divergence(pressure, open_z, 2), 1)
        updated = solve_lines(factor_y, source - divergence(middle_field, open_x, 1) - divergence(middle_field, open_z, 2), 0)
        states.append((pressure, middle_field, updated))
        pressure = updated
    back_field = adjoint_seed
    grad_source = jnp.zeros(full_shape, jnp.float32)
    face_x = jnp.zeros(full_shape, jnp.float32)
    face_y = jnp.zeros(full_shape, jnp.float32)
    face_z = jnp.zeros(full_shape, jnp.float32)
    for start_field, middle_field, updated in reversed(states):
        late_adj = solve_lines(factor_y, back_field, 0)
        early_adj = solve_lines(factor_x, -(divergence(late_adj, open_x, 1) + divergence(late_adj, open_z, 2)), 1)
        grad_source = grad_source + late_adj + early_adj
        face_x = face_x - face_product(late_adj + early_adj, middle_field, 1)
        face_y = face_y - face_product(early_adj, start_field, 0) - face_product(late_adj, updated, 0)
        face_z = face_z - face_product(early_adj, start_field, 2) - face_product(late_adj, middle_field, 2)
        back_field = -(divergence(early_adj, open_y, 0) + divergence(early_adj, open_z, 2))
    cell_sens = face_to_cells(face_x * open_x, 1) + face_to_cells(face_y * open_y, 0) + face_to_cells(face_z * open_z, 2)
    flattened = cell_sens.reshape(full_shape[0], full_shape[1] * full_shape[2])
    picked = jnp.take_along_axis(flattened, comp_cell, axis=1)
    live_mask = lax.broadcasted_iota(jnp.int32, comp_cell.shape, 1) < comp_count[:, None]
    picked = jnp.where(live_mask, picked, 0.0)
    slot_ids = well_slot[comp_well]
    well_sens = jax.ops.segment_sum(picked.reshape(-1), slot_ids.reshape(-1), num_segments=well_slot.shape[0])
    return grad_source, well_sens
```

```python
import functools

import jax
import jax.numpy as jnp
from jax import lax
from jax.experimental import pallas as pl
from jax.experimental.pallas import tpu as pltpu
from jax.sharding import PartitionSpec as P

MESH = pl.DeviceIdType.MESH
HIGHEST = lax.Precision.HIGHEST
PAD = 8

(
    T_TY, T_ST, T_SEED, T_B0, T_RW, T_B1, T_LATE1, T_P1, T_W, T_P2,
    T_PNEXT, T_FLUX, T_CELL_P, T_CELL_N, T_SLOT, T_VAL, T_MSG_P, T_MSG_N,
    T_COEF, T_S0, T_S1, T_S2, T_S3, T_R0, T_R1, T_R2, T_R3, T_PART, T_COUNT,
) = range(29)
L_SRC, L_P0, L_TX, L_TY, L_TZ, L_ST, L_COUNT = range(7)


def levels_of(extent):
    return max(1, (extent - 1).bit_length())


def kernel(
    nw, nn, nx, nk, cap, owned,
    source, pressure, trans_x, trans_y, trans_z, storage, seed, cell, well, count, slots,
    grad_out, well_out,
    src, p0, tx, ty, tz, st, p_next, flux, f_prev,
    ty_y, st_y, seed_y, b0_y, rw_y, b1_y,
    inv_y, m_y, ga_y, gb_y, late1_y, p1_y, w_y, p2_y,
    late1, p1, w_x, p2, b0, b1, rw, u0, u1, early1, early0, late0, sum0, sum1,
    gain_l, gain_r, inv_x, mid_x, ba, bb, bc,
    coef_s, coef_r, to_s, to_r, re_s, re_r,
    ia, ib, ic, pk_l, pk_r, pk_inv, tau, kap, f0s,
    cell_s, cell_r, pick_rows, onehot, lane_mask, gathered, own_v, msg_p, msg_n, msg_r,
    slot_s, slot_r, val_s, val_r, part_s, part_r,
    send_sem, recv_sem, load_sem,
):
    wi, ni = lax.axis_index("wide"), lax.axis_index("narrow")
    rows = nw * nn
    row = wi * nn + ni
    nxt, prv = lax.rem(row + 1, rows), lax.rem(row + rows - 1, rows)
    next_dev = {"wide": nxt // nn, "narrow": lax.rem(nxt, nn)}
    prev_dev = {"wide": prv // nn, "narrow": lax.rem(prv, nn)}
    xc = nx // nn
    lev, pad_x = levels_of(nx), nx // 2
    lev_w, pad_w = levels_of(nw), max(PAD, nw // 2)
    bl = min(64, nx)
    blocks = nx // bl

    barrier = pltpu.get_barrier_semaphore()

    def greet_narrow(k, c):
        pl.semaphore_signal(barrier, inc=1, device_id={"narrow": lax.rem(ni + k, nn)}, device_id_type=MESH)
        return c

    def greet_wide(k, c):
        pl.semaphore_signal(barrier, inc=1, device_id={"wide": lax.rem(wi + k, nw)}, device_id_type=MESH)
        return c

    pl.semaphore_signal(barrier, inc=1, device_id=next_dev, device_id_type=MESH)
    pl.semaphore_signal(barrier, inc=1, device_id=prev_dev, device_id_type=MESH)
    lax.fori_loop(1, nn, greet_narrow, 0)
    lax.fori_loop(1, nw, greet_wide, 0)

    loads = [
        pltpu.make_async_copy(storage, st, load_sem.at[L_ST]),
        pltpu.make_async_copy(trans_x, tx.at[pl.ds(PAD, nx)], load_sem.at[L_TX]),
        pltpu.make_async_copy(trans_y, ty, load_sem.at[L_TY]),
        pltpu.make_async_copy(pressure, p0, load_sem.at[L_P0]),
        pltpu.make_async_copy(source, src, load_sem.at[L_SRC]),
        pltpu.make_async_copy(trans_z, tz, load_sem.at[L_TZ]),
    ]
    for one in loads:
        one.start()

    def remote(from_ref, to_ref, number, device):
        return pltpu.make_async_remote_copy(
            src_ref=from_ref, dst_ref=to_ref, send_sem=send_sem.at[number], recv_sem=recv_sem.at[number],
            device_id=device, device_id_type=MESH,
        )

    def spread_narrow(number, from_of, to_ref):
        def body(k, c):
            j = lax.rem(ni + k, nn)
            remote(from_of(j), to_ref, number, {"narrow": j}).start()
            return c

        lax.fori_loop(1, nn, body, 0)
        pltpu.make_async_copy(from_of(ni), to_ref, recv_sem.at[number]).start()

    def spread_wide(number, from_ref, to_ref):
        def body(k, c):
            j = lax.rem(wi + k, nw)
            remote(from_ref.at[j], to_ref.at[wi], number, {"wide": j}).start()
            return c

        lax.fori_loop(1, nw, body, 0)
        pltpu.make_async_copy(from_ref.at[wi], to_ref.at[wi], recv_sem.at[number]).start()

    def chunk(ref):
        return lambda j: ref.at[pl.ds(pl.multiple_of(j * xc, xc), xc)]

    def to_y(number, from_ref, to_ref):
        spread_narrow(number, chunk(from_ref), to_ref.at[ni])

    def to_x(number, from_ref, to_ref):
        spread_narrow(number, lambda j: from_ref.at[j], to_ref.at[pl.ds(pl.multiple_of(PAD + ni * xc, PAD), xc)])

    def arrived(number, ref):
        pltpu.make_async_copy(ref, ref, recv_sem.at[number]).wait()

    def sent(number, ref):
        pltpu.make_async_copy(ref, ref, send_sem.at[number]).wait()

    def inner(ref):
        return ref.at[pl.ds(PAD, nx)]

    zeros_pad = jnp.zeros((PAD, nk), jnp.float32)
    for ref in (tx, late1, p1, w_x, p2, u0, u1, early1, early0, late0, sum0, sum1):
        ref[0:PAD, :] = zeros_pad
        ref[PAD + nx : 2 * PAD + nx, :] = zeros_pad
    zeros_x = jnp.zeros((pad_x, nk), jnp.float32)
    for ref in (ba, bb, bc):
        ref[0:pad_x, :] = zeros_x
        ref[pad_x + nx : 2 * pad_x + nx, :] = zeros_x
    zeros_w = jnp.zeros((pad_w, nk), jnp.float32)
    for ref in (ia, ib, ic):
        ref[0:pad_w, :] = zeros_w
        ref[pad_w + nw : 2 * pad_w + nw, :] = zeros_w
    for ref in (own_v, msg_p, msg_n):
        ref[...] = jnp.zeros_like(ref)

    cell_s[...] = jnp.zeros_like(cell_s)
    cell_s[0:1, 0:cap] = cell[...].astype(jnp.float32)

    def column(line):
        eye = lax.broadcasted_iota(jnp.int32, (cap, nk), 0) == lax.broadcasted_iota(jnp.int32, (cap, nk), 1)
        return jnp.sum(jnp.where(eye, jnp.broadcast_to(line, (cap, nk)), 0.0), axis=1, keepdims=True)

    def lanes_to_line(values):
        ones = jnp.ones((8, nk), jnp.float32)
        return lax.dot_general(
            ones, values, (((1,), (1,)), ((), ())), precision=HIGHEST, preferred_element_type=jnp.float32
        )[0:1, :]

    pick_rows[...] = jnp.zeros_like(pick_rows)
    pick_rows[0:1, 0:cap] = well[...].astype(jnp.float32)
    well_col = column(pick_rows[0:1, :])
    slot_rows = slots.shape[0]
    high = jnp.floor(well_col * (1.0 / nk))
    low = well_col - high * nk
    table_hot = jnp.where(
        jnp.broadcast_to(high, (cap, slot_rows)) == lax.broadcasted_iota(jnp.int32, (cap, slot_rows), 1).astype(jnp.float32),
        1.0, 0.0,
    )
    table = jnp.dot(table_hot, slots[...].astype(jnp.float32), precision=HIGHEST, preferred_element_type=jnp.float32)
    table = jnp.where(
        jnp.broadcast_to(low, (cap, nk)) == lax.broadcasted_iota(jnp.int32, (cap, nk), 1).astype(jnp.float32), table, 0.0
    )
    live = lax.broadcasted_iota(jnp.int32, (1, cap), 1) < count[0, 0]
    slot_s[...] = jnp.full_like(slot_s, -1.0)
    slot_s[0, 0:1, 0:cap] = jnp.where(live, lanes_to_line(table), -1.0)

    pl.semaphore_wait(barrier, nn - 1 + nw - 1 + 2)

    remote(pressure, p_next, T_PNEXT, prev_dev).start()
    to_y(T_TY, trans_y, ty_y)
    to_y(T_ST, storage, st_y)
    to_y(T_SEED, seed, seed_y)
    remote(cell_s, cell_r.at[1], T_CELL_P, prev_dev).start()
    remote(cell_s, cell_r.at[0], T_CELL_N, next_dev).start()
    spread_narrow(T_SLOT, lambda j: slot_s.at[0], slot_r.at[ni])

    def each_block(body):
        def step(i, c):
            body(pl.multiple_of(i * bl, bl))
            return c

        lax.fori_loop(0, blocks, step, 0)

    def at(ref, o, shift=0):
        return ref[pl.ds(o + shift, bl), :]

    def up(ref, o, shift=0):
        return ref[pl.ds(o + (PAD + shift), bl), :]

    def big(ref, o, shift=0):
        return ref[pl.ds(o + (pad_x + shift), bl), :]

    def next_layer(v):
        return pltpu.roll(v, nk - 1, 1)

    def prev_layer(v):
        return pltpu.roll(v, 1, 1)

    def div_z(v, o):
        f = at(tz, o) * (v - next_layer(v))
        return f - prev_layer(f)

    def div_x(ref, o):
        v = up(ref, o)
        return up(tx, o) * (v - up(ref, o, 1)) - up(tx, o, -1) * (up(ref, o, -1) - v)

    def solve_x(out):
        pair = (ba, bb)
        for level in range(lev):
            stride = 1 << level
            a, b = pair[level % 2], pair[1 - level % 2]

            def body(o):
                v = big(a, o)
                v = v + gain_l[level, pl.ds(o, bl), :] * big(a, o, -stride)
                v = v + gain_r[level, pl.ds(o, bl), :] * big(a, o, stride)
                if level == lev - 1:
                    out[pl.ds(o + PAD, bl), :] = v * at(inv_x, o)
                else:
                    b[pl.ds(o + pad_x, bl), :] = v

            each_block(body)

    def factor_x():
        def begin(o):
            t = up(tx, o)
            bb[pl.ds(o + pad_x, bl), :] = -t
            mid_x[pl.ds(o, bl), :] = at(st, o) + t + up(tx, o, -1)

        each_block(begin)
        pair = (bb, bc)
        for level in range(lev):
            stride = 1 << level
            a, b = pair[level % 2], pair[1 - level % 2]

            def invert(o):
                ba[pl.ds(o + pad_x, bl), :] = 1.0 / at(mid_x, o)

            def body(o):
                ua, ul = big(a, o), big(a, o, -stride)
                left = ul * big(ba, o, -stride)
                right = ua * big(ba, o, stride)
                gain_l[level, pl.ds(o, bl), :] = -left
                gain_r[level, pl.ds(o, bl), :] = -right
                b[pl.ds(o + pad_x, bl), :] = -right * big(a, o, stride)
                mid_x[pl.ds(o, bl), :] = at(mid_x, o) - left * ul - right * ua

            each_block(invert)
            each_block(body)

        def finish(o):
            inv_x[pl.ds(o, bl), :] = 1.0 / at(mid_x, o)

        each_block(finish)

    last = nn - 1

    def factor_y():
        def down(j, carry):
            delta, e = carry
            t = ty_y[j]
            iv = 1.0 / (delta + t)
            m = t * iv
            inv_y[j] = iv
            m_y[j] = m
            ga_y[j] = e
            return st_y[j + 1] + m * delta, m * e

        dee, kappa = lax.fori_loop(0, last, down, (st_y[0], jnp.ones((xc, nk), jnp.float32)))

        def back(i, carry):
            a, b = carry
            j = last - 1 - i
            m = m_y[j]
            a = inv_y[j] * ga_y[j] + m * a
            b = m * b
            ga_y[j] = a
            gb_y[j] = b
            return a, b

        corner, _ = lax.fori_loop(
            0, last, back, (jnp.zeros((xc, nk), jnp.float32), jnp.ones((xc, nk), jnp.float32))
        )
        t_last = jnp.where(wi == nw - 1, 0.0, ty_y[last])
        for number, value in enumerate((dee, kappa, corner, t_last)):
            coef_s[:, number, :] = value

    def reduce_y(rhs, slot):
        def body(j, carry):
            a, f = carry
            v = rhs[j]
            return a + gb_y[j] * v, f + ga_y[j] * v

        a, f = lax.fori_loop(0, last, body, (rhs[last], jnp.zeros((xc, nk), jnp.float32)))
        to_s[slot, :, 0, :] = a
        to_s[slot, :, 1, :] = f

    def inside_y(rhs, out):
        def down(j, c):
            out[j] = c
            return rhs[j + 1] + m_y[j] * c

        lax.fori_loop(0, last, down, rhs[0])

        def back(i, c):
            j = last - 1 - i
            c = inv_y[j] * out[j] + m_y[j] * c
            out[j] = c
            return c

        lax.fori_loop(0, last, back, jnp.zeros((xc, nk), jnp.float32))

    def complete_y(out, slot):
        phi = re_r[slot, :, 0, :]
        sep = re_r[slot, :, 1, :]

        def body(j, c):
            out[j] = out[j] + ga_y[j] * phi + gb_y[j] * sep
            return c

        lax.fori_loop(0, last, body, 0)
        out[last] = sep

    def mid(ref, shift=0):
        return ref[pad_w + shift : pad_w + shift + nw, :]

    def put(ref, value):
        ref[pad_w : pad_w + nw, :] = value

    def factor_sep():
        dee, kappa, corner, t_last = (coef_r[:, number, :] for number in range(4))
        put(ia, t_last)
        t_in = mid(ia, -1)
        tau_v = t_in / (1.0 + t_in * corner)
        tau[...] = tau_v
        kap[...] = kappa
        put(ia, tau_v)
        put(ib, tau_v * kappa)
        middle = dee + mid(ia, 1) + kappa * kappa * tau_v
        upper = -mid(ib, 1)
        for level in range(lev_w):
            stride = 1 << level
            put(ia, 1.0 / middle)
            put(ib, upper)
            lower = mid(ib, -stride)
            left = lower * mid(ia, -stride)
            right = upper * mid(ia, stride)
            pk_l[level] = -left
            pk_r[level] = -right
            middle = middle - left * lower - right * upper
            upper = -right * mid(ib, stride)
        pk_inv[...] = 1.0 / middle

    def solve_sep(slot):
        alpha = to_r[slot, :, 0, :]
        f0 = to_r[slot, :, 1, :]
        tf = tau[...] * f0
        put(ic, tf)
        v = alpha + mid(ic, 1) - kap[...] * tf
        for level in range(lev_w):
            stride = 1 << level
            ref = (ia, ib)[level % 2]
            put(ref, v)
            v = v + pk_l[level] * mid(ref, -stride) + pk_r[level] * mid(ref, stride)
        v = v * pk_inv[...]
        put(ic, v)
        re_s[slot, :, 0, :] = tau[...] * (mid(ic, -1) - f0 - kap[...] * v)
        re_s[slot, :, 1, :] = v

    def prepare_picks():
        for number, line in enumerate((cell_s[0:1, :], cell_r[0], cell_r[1])):
            col = column(line)
            x_of = jnp.floor(col * (1.0 / nk))
            layer = col - x_of * nk
            rows_at = pl.ds(number * cap, cap)
            onehot[rows_at, :] = jnp.where(
                jnp.broadcast_to(x_of, (cap, nx)) == lax.broadcasted_iota(jnp.int32, (cap, nx), 1).astype(jnp.float32), 1.0, 0.0
            )
            lane_mask[rows_at, :] = jnp.where(
                jnp.broadcast_to(layer, (cap, nk)) == lax.broadcasted_iota(jnp.int32, (cap, nk), 1).astype(jnp.float32), 1.0, 0.0
            )

    def pick(number, values):
        gathered[...] = lane_mask[...] * jnp.dot(
            onehot[...], values, precision=HIGHEST, preferred_element_type=jnp.float32
        )
        own_v[number : number + 1, 0:cap] = lanes_to_line(gathered[0:cap, :])
        if number < 7:
            msg_p[number : number + 1, 0:cap] = lanes_to_line(gathered[cap : 2 * cap, :])
            msg_n[number : number + 1, 0:cap] = lanes_to_line(gathered[2 * cap : 3 * cap, :])

    loads[0].wait()
    loads[1].wait()
    tx[PAD + nx - 1 : PAD + nx, :] = jnp.zeros((1, nk), jnp.float32)
    factor_x()

    for one in loads[2:]:
        one.wait()
    lane = lax.broadcasted_iota(jnp.int32, (bl, nk), 1)
    open_y = row < rows - 1

    arrived(T_PNEXT, p_next)

    def make_flux(o):
        tz[pl.ds(o, bl), :] = jnp.where(lane < nk - 1, at(tz, o), 0.0)
        t = jnp.where(open_y, at(ty, o), 0.0)
        ty[pl.ds(o, bl), :] = t
        flux[pl.ds(o, bl), :] = t * (at(p0, o) - at(p_next, o))

    each_block(make_flux)
    remote(flux, f_prev, T_FLUX, next_dev).start()

    arrived(T_TY, ty_y)
    arrived(T_ST, st_y)
    factor_y()
    spread_wide(T_COEF, coef_s, coef_r)

    def start_y(rhs, number, slot, out):
        arrived(number, rhs)
        reduce_y(rhs, slot)
        spread_wide(T_S0 + slot, to_s.at[slot], to_r.at[slot])
        inside_y(rhs, out)

    def middle_y(slot):
        arrived(T_S0 + slot, to_r.at[slot])
        solve_sep(slot)
        spread_wide(T_R0 + slot, re_s.at[slot], re_r.at[slot])

    def end_y(slot, out, number, to_ref):
        arrived(T_R0 + slot, re_r.at[slot])
        complete_y(out, slot)
        to_x(number, out, to_ref)

    start_y(seed_y, T_SEED, 0, late1_y)

    arrived(T_FLUX, f_prev)

    def rhs_u0(o):
        ba[pl.ds(o + pad_x, bl), :] = at(src, o) - (at(flux, o) - at(f_prev, o)) - div_z(at(p0, o), o)

    each_block(rhs_u0)
    solve_x(u0)

    def make_b0(o):
        b0[pl.ds(o, bl), :] = at(src, o) - div_x(u0, o) - div_z(up(u0, o), o)

    each_block(make_b0)
    to_y(T_B0, b0, b0_y)

    arrived(T_COEF, coef_r)
    factor_sep()
    middle_y(0)

    arrived(T_CELL_P, cell_r.at[1])
    arrived(T_CELL_N, cell_r.at[0])
    prepare_picks()
    end_y(0, late1_y, T_LATE1, late1)

    start_y(b0_y, T_B0, 1, p1_y)
    pick(1, p0[...])
    pick(6, ty[...])
    middle_y(1)

    arrived(T_LATE1, inner(late1))

    def rhs_early(ref):
        def body(o):
            ba[pl.ds(o + pad_x, bl), :] = -(div_x(ref, o) + div_z(up(ref, o), o))

        each_block(body)

    rhs_early(late1)
    solve_x(early1)

    def make_rw(o):
        v = up(early1, o)
        rw[pl.ds(o, bl), :] = at(st, o) * v - div_z(v, o)

    each_block(make_rw)
    to_y(T_RW, rw, rw_y)
    end_y(1, p1_y, T_P1, p1)
    pick(4, late1[PAD : PAD + nx, :])

    start_y(rw_y, T_RW, 2, w_y)

    arrived(T_P1, inner(p1))

    def rhs_u1(o):
        v = up(p1, o)
        ba[pl.ds(o + pad_x, bl), :] = at(src, o) - at(b0, o) + at(st, o) * v - div_z(v, o)

    each_block(rhs_u1)
    solve_x(u1)

    def make_b1(o):
        b1[pl.ds(o, bl), :] = at(src, o) - div_x(u1, o) - div_z(up(u1, o), o)

    each_block(make_b1)
    to_y(T_B1, b1, b1_y)

    middle_y(2)
    pick(3, p1[PAD : PAD + nx, :])
    end_y(2, w_y, T_W, w_x)

    start_y(b1_y, T_B1, 3, p2_y)
    middle_y(3)

    arrived(T_W, inner(w_x))

    def make_late0(o):
        late0[pl.ds(o + PAD, bl), :] = up(w_x, o) - up(early1, o)

    each_block(make_late0)
    end_y(3, p2_y, T_P2, p2)
    rhs_early(late0)
    solve_x(early0)

    def make_sums(o):
        sum0[pl.ds(o + PAD, bl), :] = up(late0, o) + up(early0, o)
        both = up(late1, o) + up(early1, o)
        sum1[pl.ds(o + PAD, bl), :] = both
        grad_out[pl.ds(o, bl), :] = up(w_x, o) + up(early0, o) + up(late1, o)

    each_block(make_sums)

    def face_x(o):
        a = (up(sum0, o) - up(sum0, o, 1)) * (up(u0, o) - up(u0, o, 1))
        b = (up(sum1, o) - up(sum1, o, 1)) * (up(u1, o) - up(u1, o, 1))
        ba[pl.ds(o + pad_x, bl), :] = up(tx, o) * (a + b)

    each_block(face_x)

    def step_z(v):
        return v - next_layer(v)

    def cells_xz(o):
        z = step_z(up(early0, o)) * step_z(at(p0, o)) + step_z(up(late0, o)) * step_z(up(u0, o))
        z = z + step_z(up(early1, o)) * step_z(up(p1, o)) + step_z(up(late1, o)) * step_z(up(u1, o))
        z = at(tz, o) * z
        bb[pl.ds(o + pad_x, bl), :] = -0.5 * (big(ba, o) + big(ba, o, -1)) - 0.5 * (z + prev_layer(z))

    each_block(cells_xz)
    pick(7, bb[pad_x : pad_x + nx, :])
    pick(0, early0[PAD : PAD + nx, :])
    pick(2, w_x[PAD : PAD + nx, :])
    arrived(T_P2, inner(p2))
    pick(5, p2[PAD : PAD + nx, :])
    remote(msg_p, msg_r.at[1], T_MSG_P, prev_dev).start()
    remote(msg_n, msg_r.at[0], T_MSG_N, next_dev).start()
    arrived(T_MSG_P, msg_r.at[1])
    arrived(T_MSG_N, msg_r.at[0])

    before = msg_r[0] - own_v[...]
    after = own_v[...] - msg_r[1]

    def pairs(d):
        return d[0:1] * d[1:2] + d[2:3] * d[3:4] + d[4:5] * d[5:6]

    val_s[0] = own_v[7:8, :] - 0.5 * (own_v[6:7, :] * pairs(after) + msg_r[0, 6:7, :] * pairs(before))
    arrived(T_SLOT, slot_r)
    spread_narrow(T_VAL, lambda j: val_s.at[0], val_r.at[ni])
    arrived(T_VAL, val_r)

    base = ((lax.broadcasted_iota(jnp.int32, (nw, nk), 0) * nn + ni) * owned).astype(jnp.float32)
    within = lax.broadcasted_iota(jnp.int32, (nk, nk), 0).astype(jnp.float32)

    def add_terms(i, total):
        s = slot_r[i]
        v = val_r[i]
        rest = s - owned * jnp.floor((s + 0.5) * (1.0 / owned))
        s_all = jnp.broadcast_to(s, (nw, nk))
        a = jnp.where((s_all >= base) & (s_all < base + owned), jnp.broadcast_to(v, (nw, nk)), 0.0)
        b = jnp.where(jnp.broadcast_to(rest, (nk, nk)) == within, 1.0, 0.0)
        return total + lax.dot_general(
            a, b, (((1,), (1,)), ((), ())), precision=HIGHEST, preferred_element_type=jnp.float32
        )

    part_s[:, 0, :] = lax.fori_loop(0, nn, add_terms, jnp.zeros((nw, nk), jnp.float32))
    spread_wide(T_PART, part_s, part_r)
    arrived(T_PART, part_r)
    well_out[...] = jnp.sum(part_r[...], axis=0)

    for number in (T_TY, T_ST, T_SEED, T_B0, T_RW, T_B1, T_LATE1, T_P1, T_W, T_P2):
        sent(number, ty_y.at[pl.ds(0, nn - 1)])
    sent(T_PNEXT, p_next)
    sent(T_FLUX, flux)
    sent(T_CELL_P, cell_s)
    sent(T_CELL_N, cell_s)
    sent(T_MSG_P, msg_p)
    sent(T_MSG_N, msg_n)
    sent(T_SLOT, slot_r.at[pl.ds(0, nn - 1)])
    sent(T_VAL, slot_r.at[pl.ds(0, nn - 1)])
    sent(T_COEF, coef_s.at[pl.ds(0, nw - 1)])
    for slot in range(4):
        sent(T_S0 + slot, to_s.at[slot, pl.ds(0, nw - 1)])
        sent(T_R0 + slot, re_s.at[slot, pl.ds(0, nw - 1)])
    sent(T_PART, part_s.at[pl.ds(0, nw - 1)])


def local(
    source, pressure_start, trans_x, trans_y, trans_z, storage, adjoint_seed,
    comp_cell, comp_well, comp_count, well_slot,
):
    _, nx, nk = source.shape
    nw, nn = lax.axis_size("wide"), lax.axis_size("narrow")
    cap = comp_cell.shape[1]
    owned = well_slot.shape[0] // (nw * nn)
    xc = nx // nn
    pad_w = max(PAD, nw // 2)
    f32 = jnp.float32

    def plain():
        return pltpu.VMEM((nx, nk), f32)

    def padded():
        return pltpu.VMEM((nx + 2 * PAD, nk), f32)

    def wide_pad():
        return pltpu.VMEM((2 * nx, nk), f32)

    def block():
        return pltpu.VMEM((nn, xc, nk), f32)

    def sep_pad():
        return pltpu.VMEM((nw + 2 * pad_w, nk), f32)

    def sep():
        return pltpu.VMEM((nw, nk), f32)

    def many(make, number):
        return [make() for _ in range(number)]

    scratch = (
        [plain(), plain(), padded()] + many(plain, 6)
        + many(block, 6) + many(block, 8)
        + many(padded, 4) + many(plain, 3) + many(padded, 7)
        + [pltpu.VMEM((levels_of(nx), nx, nk), f32)] * 2 + many(plain, 2) + many(wide_pad, 3)
        + [pltpu.VMEM((nw, 4, nk), f32)] * 2 + [pltpu.VMEM((4, nw, 2, nk), f32)] * 4
        + many(sep_pad, 3) + [pltpu.VMEM((levels_of(nw), nw, nk), f32)] * 2 + many(sep, 4)
        + [pltpu.VMEM((1, nk), f32), pltpu.VMEM((2, 1, nk), f32), pltpu.VMEM((8, nk), f32)]
        + [pltpu.VMEM((3 * cap, nx), f32), pltpu.VMEM((3 * cap, nk), f32), pltpu.VMEM((3 * cap, nk), f32)]
        + [pltpu.VMEM((8, nk), f32)] * 3 + [pltpu.VMEM((2, 8, nk), f32)]
        + [pltpu.VMEM((1, 1, nk), f32), pltpu.VMEM((nn, 1, nk), f32)] * 2
        + [pltpu.VMEM((nw, 1, nk), f32)] * 2
        + [pltpu.SemaphoreType.DMA((T_COUNT,)), pltpu.SemaphoreType.DMA((T_COUNT,)), pltpu.SemaphoreType.DMA((L_COUNT,))]
    )
    hbm = pl.BlockSpec(memory_space=pl.ANY)
    vmem = pl.BlockSpec(memory_space=pltpu.VMEM)
    smem = pl.BlockSpec(memory_space=pltpu.SMEM)
    grad, sums = pl.pallas_call(
        functools.partial(kernel, nw, nn, nx, nk, cap, owned),
        out_shape=(jax.ShapeDtypeStruct((nx, nk), f32), jax.ShapeDtypeStruct((1, nk), f32)),
        in_specs=[hbm] * 7 + [vmem, vmem, smem, vmem],
        out_specs=(vmem, vmem),
        scratch_shapes=scratch,
        compiler_params=pltpu.CompilerParams(
            collective_id=0, has_side_effects=True, vmem_limit_bytes=48 * 1024 * 1024
        ),
    )(
        source[0], pressure_start[0], trans_x[0], trans_y[0], trans_z[0], storage[0], adjoint_seed[0],
        comp_cell, comp_well, comp_count.reshape(1, 1), well_slot.reshape(-1, nk),
    )
    return grad[None], sums[0, :owned]


def solution(mesh):
    cells = P(("wide", "narrow"), None, None)
    placed = (cells,) * 7 + (P(("wide", "narrow"), None), P(("wide", "narrow"), None), P(("wide", "narrow")), P())
    return jax.shard_map(
        local, mesh=mesh, in_specs=placed, out_specs=(cells, P(("wide", "narrow"))), check_vma=False
    )
```

```python
import functools

import jax
import jax.numpy as jnp
from jax import lax
from jax.experimental import pallas as pl
from jax.experimental.pallas import tpu as pltpu
from jax.sharding import PartitionSpec as P

MESH = pl.DeviceIdType.MESH
HIGHEST = lax.Precision.HIGHEST
PAD = 8

(
    T_TY, T_ST, T_SEED, T_B0, T_RW, T_B1, T_LATE1, T_P1, T_W, T_TIN,
    T_PNEXT, T_FLUX, T_CELL_P, T_CELL_N, T_SLOT, T_VAL, T_MSG_P, T_MSG_N,
    T_COEF, T_S0, T_S1, T_S2, T_S3, T_R0, T_R1, T_R2, T_R3, T_PART, T_COUNT,
) = range(29)
L_SRC, L_P0, L_TX, L_TY, L_TZ, L_ST, L_COUNT = range(7)


def levels_of(extent):
    return max(1, (extent - 1).bit_length())


def kernel(
    nw, nn, nx, nk, cap, owned,
    source, pressure, trans_x, trans_y, trans_z, storage, seed, cell, well, count, slots,
    grad_out, well_out,
    src, p0, tx, ty, tz, st, p_next, flux, f_prev,
    ty_y, st_y, seed_y, b0_y, rw_y, b1_y,
    inv_y, m_y, ga_y, gb_y, late1_y, p1_y, w_y, p2_y,
    late1, p1, w_x, b0, b1, rw, u0, u1, early1, early0, late0, sum0, sum1,
    gain_l, gain_r, inv_x, mid_x, ba, bb, bc,
    coef_s, coef_r, to_s, to_r, re_s, re_r,
    ia, ib, ic, pk_l, pk_r, pk_inv, tau, kap, f0s,
    cell_s, cell_r, pick_rows, onehot, lane_mask, gathered, own_v, msg_p, msg_n, msg_r,
    slot_s, slot_r, val_s, val_r, part_s, part_r,
    tin_s, tin_r, c_y, hot_y, mask_y, picked_y, slot_line, owner_hot, place_hot,
    send_sem, recv_sem, load_sem,
):
    wi, ni = lax.axis_index("wide"), lax.axis_index("narrow")
    rows = nw * nn
    row = wi * nn + ni
    nxt, prv = lax.rem(row + 1, rows), lax.rem(row + rows - 1, rows)
    next_dev = {"wide": nxt // nn, "narrow": lax.rem(nxt, nn)}
    prev_dev = {"wide": prv // nn, "narrow": lax.rem(prv, nn)}
    xc = nx // nn
    lev, pad_x = levels_of(nx), nx // 2
    lev_w, pad_w = levels_of(nw), max(PAD, nw // 2)
    bl = min(64, nx)
    blocks = nx // bl

    barrier = pltpu.get_barrier_semaphore()

    def greet_narrow(k, c):
        pl.semaphore_signal(barrier, inc=1, device_id={"narrow": lax.rem(ni + k, nn)}, device_id_type=MESH)
        return c

    def greet_wide(k, c):
        pl.semaphore_signal(barrier, inc=1, device_id={"wide": lax.rem(wi + k, nw)}, device_id_type=MESH)
        return c

    pl.semaphore_signal(barrier, inc=1, device_id=next_dev, device_id_type=MESH)
    pl.semaphore_signal(barrier, inc=1, device_id=prev_dev, device_id_type=MESH)
    lax.fori_loop(1, nn, greet_narrow, 0)
    lax.fori_loop(1, nw, greet_wide, 0)

    loads = [
        pltpu.make_async_copy(storage, st, load_sem.at[L_ST]),
        pltpu.make_async_copy(trans_x, tx.at[pl.ds(PAD, nx)], load_sem.at[L_TX]),
        pltpu.make_async_copy(trans_y, ty, load_sem.at[L_TY]),
        pltpu.make_async_copy(pressure, p0, load_sem.at[L_P0]),
        pltpu.make_async_copy(source, src, load_sem.at[L_SRC]),
        pltpu.make_async_copy(trans_z, tz, load_sem.at[L_TZ]),
    ]
    for one in loads:
        one.start()

    def remote(from_ref, to_ref, number, device):
        return pltpu.make_async_remote_copy(
            src_ref=from_ref, dst_ref=to_ref, send_sem=send_sem.at[number], recv_sem=recv_sem.at[number],
            device_id=device, device_id_type=MESH,
        )

    def spread_narrow(number, from_of, to_ref):
        def body(k, c):
            j = lax.rem(ni + k, nn)
            remote(from_of(j), to_ref, number, {"narrow": j}).start()
            return c

        lax.fori_loop(1, nn, body, 0)
        pltpu.make_async_copy(from_of(ni), to_ref, recv_sem.at[number]).start()

    def spread_wide(number, from_ref, to_ref):
        def body(k, c):
            j = lax.rem(wi + k, nw)
            remote(from_ref.at[j], to_ref.at[wi], number, {"wide": j}).start()
            return c

        lax.fori_loop(1, nw, body, 0)
        pltpu.make_async_copy(from_ref.at[wi], to_ref.at[wi], recv_sem.at[number]).start()

    def chunk(ref):
        return lambda j: ref.at[pl.ds(pl.multiple_of(j * xc, xc), xc)]

    def to_y(number, from_ref, to_ref):
        spread_narrow(number, chunk(from_ref), to_ref.at[ni])

    def to_x(number, from_ref, to_ref):
        spread_narrow(number, lambda j: from_ref.at[j], to_ref.at[pl.ds(pl.multiple_of(PAD + ni * xc, PAD), xc)])

    def arrived(number, ref):
        pltpu.make_async_copy(ref, ref, recv_sem.at[number]).wait()

    def sent(number, ref):
        pltpu.make_async_copy(ref, ref, send_sem.at[number]).wait()

    def inner(ref):
        return ref.at[pl.ds(PAD, nx)]

    zeros_pad = jnp.zeros((PAD, nk), jnp.float32)
    for ref in (tx, late1, p1, w_x, u0, u1, early1, early0, late0, sum0, sum1):
        ref[0:PAD, :] = zeros_pad
        ref[PAD + nx : 2 * PAD + nx, :] = zeros_pad
    zeros_x = jnp.zeros((pad_x, nk), jnp.float32)
    for ref in (ba, bb, bc):
        ref[0:pad_x, :] = zeros_x
        ref[pad_x + nx : 2 * pad_x + nx, :] = zeros_x
    zeros_w = jnp.zeros((pad_w, nk), jnp.float32)
    for ref in (ia, ib, ic):
        ref[0:pad_w, :] = zeros_w
        ref[pad_w + nw : 2 * pad_w + nw, :] = zeros_w
    for ref in (own_v, msg_p, msg_n):
        ref[...] = jnp.zeros_like(ref)

    cell_s[...] = jnp.zeros_like(cell_s)
    cell_s[0:1, 0:cap] = cell[...].astype(jnp.float32)

    def column(line):
        eye = lax.broadcasted_iota(jnp.int32, (cap, nk), 0) == lax.broadcasted_iota(jnp.int32, (cap, nk), 1)
        return jnp.sum(jnp.where(eye, jnp.broadcast_to(line, (cap, nk)), 0.0), axis=1, keepdims=True)

    def lanes_to_line(values):
        ones = jnp.ones((8, nk), jnp.float32)
        return lax.dot_general(
            ones, values, (((1,), (1,)), ((), ())), precision=HIGHEST, preferred_element_type=jnp.float32
        )[0:1, :]

    pick_rows[...] = jnp.zeros_like(pick_rows)
    pick_rows[0:1, 0:cap] = well[...].astype(jnp.float32)
    well_col = column(pick_rows[0:1, :])
    slot_rows = slots.shape[0]
    high = jnp.floor(well_col * (1.0 / nk))
    low = well_col - high * nk
    table_hot = jnp.where(
        jnp.broadcast_to(high, (cap, slot_rows)) == lax.broadcasted_iota(jnp.int32, (cap, slot_rows), 1).astype(jnp.float32),
        1.0, 0.0,
    )
    table = jnp.dot(table_hot, slots[...].astype(jnp.float32), precision=HIGHEST, preferred_element_type=jnp.float32)
    table = jnp.where(
        jnp.broadcast_to(low, (cap, nk)) == lax.broadcasted_iota(jnp.int32, (cap, nk), 1).astype(jnp.float32), table, 0.0
    )
    live = lax.broadcasted_iota(jnp.int32, (1, cap), 1) < count[0, 0]
    slot_s[...] = jnp.full_like(slot_s, -1.0)
    slot_s[0, 0:1, 0:cap] = jnp.where(live, lanes_to_line(table), -1.0)
    slot_s[0, 1:2, 0:cap] = cell_s[0:1, 0:cap]

    pl.semaphore_wait(barrier, nn - 1 + nw - 1 + 2)

    to_y(T_TY, trans_y, ty_y)
    to_y(T_ST, storage, st_y)
    remote(pressure, p_next, T_PNEXT, prev_dev).start()
    to_y(T_SEED, seed, seed_y)
    remote(cell_s, cell_r.at[1], T_CELL_P, prev_dev).start()
    remote(cell_s, cell_r.at[0], T_CELL_N, next_dev).start()
    spread_narrow(T_SLOT, lambda j: slot_s.at[0], slot_r.at[ni])

    def each_block(body):
        def step(i, c):
            body(pl.multiple_of(i * bl, bl))
            return c

        lax.fori_loop(0, blocks, step, 0)

    def at(ref, o, shift=0):
        return ref[pl.ds(o + shift, bl), :]

    def up(ref, o, shift=0):
        return ref[pl.ds(o + (PAD + shift), bl), :]

    def big(ref, o, shift=0):
        return ref[pl.ds(o + (pad_x + shift), bl), :]

    def next_layer(v):
        return pltpu.roll(v, nk - 1, 1)

    def prev_layer(v):
        return pltpu.roll(v, 1, 1)

    def div_z(v, o):
        f = at(tz, o) * (v - next_layer(v))
        return f - prev_layer(f)

    def div_x(ref, o):
        v = up(ref, o)
        return up(tx, o) * (v - up(ref, o, 1)) - up(tx, o, -1) * (up(ref, o, -1) - v)

    def solve_x(out):
        pair = (ba, bb)
        for level in range(lev):
            stride = 1 << level
            a, b = pair[level % 2], pair[1 - level % 2]

            def body(o):
                v = big(a, o)
                v = v + gain_l[level, pl.ds(o, bl), :] * big(a, o, -stride)
                v = v + gain_r[level, pl.ds(o, bl), :] * big(a, o, stride)
                if level == lev - 1:
                    out[pl.ds(o + PAD, bl), :] = v * at(inv_x, o)
                else:
                    b[pl.ds(o + pad_x, bl), :] = v

            each_block(body)

    def factor_x():
        def begin(o):
            t = up(tx, o)
            bb[pl.ds(o + pad_x, bl), :] = -t
            mid_x[pl.ds(o, bl), :] = at(st, o) + t + up(tx, o, -1)

        each_block(begin)
        pair = (bb, bc)
        for level in range(lev):
            stride = 1 << level
            a, b = pair[level % 2], pair[1 - level % 2]

            def invert(o):
                ba[pl.ds(o + pad_x, bl), :] = 1.0 / at(mid_x, o)

            def body(o):
                ua, ul = big(a, o), big(a, o, -stride)
                left = ul * big(ba, o, -stride)
                right = ua * big(ba, o, stride)
                gain_l[level, pl.ds(o, bl), :] = -left
                gain_r[level, pl.ds(o, bl), :] = -right
                b[pl.ds(o + pad_x, bl), :] = -right * big(a, o, stride)
                mid_x[pl.ds(o, bl), :] = at(mid_x, o) - left * ul - right * ua

            each_block(invert)
            each_block(body)

        def finish(o):
            inv_x[pl.ds(o, bl), :] = 1.0 / at(mid_x, o)

        each_block(finish)

    last = nn - 1

    def factor_y():
        def down(j, carry):
            delta, e = carry
            t = ty_y[j]
            iv = 1.0 / (delta + t)
            m = t * iv
            inv_y[j] = iv
            m_y[j] = m
            ga_y[j] = e
            return st_y[j + 1] + m * delta, m * e

        dee, kappa = lax.fori_loop(0, last, down, (st_y[0], jnp.ones((xc, nk), jnp.float32)))

        def back(i, carry):
            a, b = carry
            j = last - 1 - i
            m = m_y[j]
            a = inv_y[j] * ga_y[j] + m * a
            b = m * b
            ga_y[j] = a
            gb_y[j] = b
            return a, b

        corner, _ = lax.fori_loop(
            0, last, back, (jnp.zeros((xc, nk), jnp.float32), jnp.ones((xc, nk), jnp.float32))
        )
        t_last = jnp.where(wi == nw - 1, 0.0, ty_y[last])
        for number, value in enumerate((dee, kappa, corner, t_last)):
            coef_s[:, number, :] = value

    def reduce_y(rhs, slot):
        def body(j, carry):
            a, f = carry
            v = rhs[j]
            return a + gb_y[j] * v, f + ga_y[j] * v

        a, f = lax.fori_loop(0, last, body, (rhs[last], jnp.zeros((xc, nk), jnp.float32)))
        to_s[slot, :, 0, :] = a
        to_s[slot, :, 1, :] = f

    def inside_y(rhs, out):
        def down(j, c):
            out[j] = c
            return rhs[j + 1] + m_y[j] * c

        lax.fori_loop(0, last, down, rhs[0])

        def back(i, c):
            j = last - 1 - i
            c = inv_y[j] * out[j] + m_y[j] * c
            out[j] = c
            return c

        lax.fori_loop(0, last, back, jnp.zeros((xc, nk), jnp.float32))

    def complete_y(out, slot):
        phi = re_r[slot, :, 0, :]
        sep = re_r[slot, :, 1, :]

        def body(j, c):
            out[j] = out[j] + ga_y[j] * phi + gb_y[j] * sep
            return c

        lax.fori_loop(0, last, body, 0)
        out[last] = sep

    def mid(ref, shift=0):
        return ref[pad_w + shift : pad_w + shift + nw, :]

    def put(ref, value):
        ref[pad_w : pad_w + nw, :] = value

    def factor_sep():
        dee, kappa, corner, t_last = (coef_r[:, number, :] for number in range(4))
        put(ia, t_last)
        t_in = mid(ia, -1)
        tau_v = t_in / (1.0 + t_in * corner)
        tau[...] = tau_v
        kap[...] = kappa
        tin_s[:, 0, :] = t_in
        put(ia, tau_v)
        put(ib, tau_v * kappa)
        middle = dee + mid(ia, 1) + kappa * kappa * tau_v
        upper = -mid(ib, 1)
        for level in range(lev_w):
            stride = 1 << level
            put(ia, 1.0 / middle)
            put(ib, upper)
            lower = mid(ib, -stride)
            left = lower * mid(ia, -stride)
            right = upper * mid(ia, stride)
            pk_l[level] = -left
            pk_r[level] = -right
            middle = middle - left * lower - right * upper
            upper = -right * mid(ib, stride)
        pk_inv[...] = 1.0 / middle

    def solve_sep(slot):
        alpha = to_r[slot, :, 0, :]
        f0 = to_r[slot, :, 1, :]
        tf = tau[...] * f0
        put(ic, tf)
        v = alpha + mid(ic, 1) - kap[...] * tf
        for level in range(lev_w):
            stride = 1 << level
            ref = (ia, ib)[level % 2]
            put(ref, v)
            v = v + pk_l[level] * mid(ref, -stride) + pk_r[level] * mid(ref, stride)
        v = v * pk_inv[...]
        put(ic, v)
        re_s[slot, :, 0, :] = tau[...] * (mid(ic, -1) - f0 - kap[...] * v)
        re_s[slot, :, 1, :] = v

    def prepare_picks():
        for number, line in enumerate((cell_s[0:1, :], cell_r[0], cell_r[1])):
            col = column(line)
            x_of = jnp.floor(col * (1.0 / nk))
            layer = col - x_of * nk
            rows_at = pl.ds(number * cap, cap)
            onehot[rows_at, :] = jnp.where(
                jnp.broadcast_to(x_of, (cap, nx)) == lax.broadcasted_iota(jnp.int32, (cap, nx), 1).astype(jnp.float32), 1.0, 0.0
            )
            lane_mask[rows_at, :] = jnp.where(
                jnp.broadcast_to(layer, (cap, nk)) == lax.broadcasted_iota(jnp.int32, (cap, nk), 1).astype(jnp.float32), 1.0, 0.0
            )

    def pick(number, values):
        gathered[...] = lane_mask[...] * jnp.dot(
            onehot[...], values, precision=HIGHEST, preferred_element_type=jnp.float32
        )
        own_v[number : number + 1, 0:cap] = lanes_to_line(gathered[0:cap, :])
        if number < 7:
            msg_p[number : number + 1, 0:cap] = lanes_to_line(gathered[cap : 2 * cap, :])
            msg_n[number : number + 1, 0:cap] = lanes_to_line(gathered[2 * cap : 3 * cap, :])

    terms = nn * cap

    def prepare_group():
        arrived(T_SLOT, slot_r)
        for j in range(nn):
            slot_line[0:1, j * cap : (j + 1) * cap] = slot_r[j, 0:1, 0:cap]

        def body(j, c):
            col = column(slot_r[j, 1:2, :])
            x_of = jnp.floor(col * (1.0 / nk))
            layer = col - x_of * nk
            x_of = x_of - (ni * xc).astype(jnp.float32)
            hot_y[j] = jnp.where(
                jnp.broadcast_to(x_of, (cap, xc)) == lax.broadcasted_iota(jnp.int32, (cap, xc), 1).astype(jnp.float32), 1.0, 0.0
            )
            mask_y[j] = jnp.where(
                jnp.broadcast_to(layer, (cap, nk)) == lax.broadcasted_iota(jnp.int32, (cap, nk), 1).astype(jnp.float32), 1.0, 0.0
            )
            return c

        lax.fori_loop(0, nn, body, 0)

    def prepare_owners():
        s_line = slot_line[...]
        base = ((lax.broadcasted_iota(jnp.int32, (nw, terms), 0) * nn + ni) * owned).astype(jnp.float32)
        s_all = jnp.broadcast_to(s_line, (nw, terms))
        owner_hot[...] = jnp.where((s_all >= base) & (s_all < base + owned), 1.0, 0.0)
        rest = s_line - owned * jnp.floor((s_line + 0.5) * (1.0 / owned))
        place_hot[...] = jnp.where(
            jnp.broadcast_to(rest, (nk, terms)) == lax.broadcasted_iota(jnp.int32, (nk, terms), 0).astype(jnp.float32), 1.0, 0.0
        )

    def cells_y():
        t_in = tin_r[:, 0, :]
        there = t_in > 0.0
        e0 = jnp.where(there, re_r[0, :, 0, :] * re_r[3, :, 0, :] / jnp.where(there, t_in, 1.0), 0.0)

        def body(j, before):
            e = ty_y[j] * (late1_y[j] - late1_y[j + 1]) * (p2_y[j] - p2_y[j + 1])
            c_y[j] = -0.5 * (e + before)
            return e

        before = lax.fori_loop(0, last, body, e0)

        def out_flux(rhs, v):
            return rhs[last] - st_y[last] * v[last] - ty_y[last - 1] * (v[last] - v[last - 1])

        e = jnp.where(wi == nw - 1, 0.0, out_flux(seed_y, late1_y) * out_flux(b1_y, p2_y) / ty_y[last])
        c_y[last] = -0.5 * (e + before)

    def pick_y():
        for j in range(nn):
            picked_y[j * cap : (j + 1) * cap, :] = mask_y[j] * jnp.dot(
                hot_y[j], c_y[j], precision=HIGHEST, preferred_element_type=jnp.float32
            )
        return lanes_to_line(picked_y[...])

    def start_y(rhs, number, slot, out):
        arrived(number, rhs)
        reduce_y(rhs, slot)
        spread_wide(T_S0 + slot, to_s.at[slot], to_r.at[slot])
        inside_y(rhs, out)

    def middle_y(slot):
        arrived(T_S0 + slot, to_r.at[slot])
        solve_sep(slot)
        spread_wide(T_R0 + slot, re_s.at[slot], re_r.at[slot])

    def end_y(slot, out, number=None, to_ref=None):
        arrived(T_R0 + slot, re_r.at[slot])
        complete_y(out, slot)
        if number is not None:
            to_x(number, out, to_ref)

    loads[0].wait()
    loads[1].wait()
    tx[PAD + nx - 1 : PAD + nx, :] = jnp.zeros((1, nk), jnp.float32)
    factor_x()
    for one in loads[2:]:
        one.wait()
    lane = lax.broadcasted_iota(jnp.int32, (bl, nk), 1)
    open_y = row < rows - 1

    arrived(T_TY, ty_y)
    arrived(T_ST, st_y)
    factor_y()
    spread_wide(T_COEF, coef_s, coef_r)

    arrived(T_PNEXT, p_next)

    def make_flux(o):
        tz[pl.ds(o, bl), :] = jnp.where(lane < nk - 1, at(tz, o), 0.0)
        t = jnp.where(open_y, at(ty, o), 0.0)
        ty[pl.ds(o, bl), :] = t
        flux[pl.ds(o, bl), :] = t * (at(p0, o) - at(p_next, o))

    each_block(make_flux)
    remote(flux, f_prev, T_FLUX, next_dev).start()

    start_y(seed_y, T_SEED, 0, late1_y)

    arrived(T_CELL_P, cell_r.at[1])
    arrived(T_CELL_N, cell_r.at[0])
    prepare_picks()

    arrived(T_FLUX, f_prev)

    def rhs_u0(o):
        ba[pl.ds(o + pad_x, bl), :] = at(src, o) - (at(flux, o) - at(f_prev, o)) - div_z(at(p0, o), o)

    each_block(rhs_u0)
    solve_x(u0)

    def make_b0(o):
        b0[pl.ds(o, bl), :] = at(src, o) - div_x(u0, o) - div_z(up(u0, o), o)

    each_block(make_b0)
    to_y(T_B0, b0, b0_y)

    arrived(T_COEF, coef_r)
    factor_sep()
    middle_y(0)
    spread_wide(T_TIN, tin_s, tin_r)

    start_y(b0_y, T_B0, 1, p1_y)
    pick(1, p0[...])
    end_y(0, late1_y, T_LATE1, late1)
    pick(6, ty[...])
    middle_y(1)

    arrived(T_LATE1, inner(late1))

    def rhs_early(ref):
        def body(o):
            ba[pl.ds(o + pad_x, bl), :] = -(div_x(ref, o) + div_z(up(ref, o), o))

        each_block(body)

    rhs_early(late1)
    solve_x(early1)

    def make_rw(o):
        v = up(early1, o)
        rw[pl.ds(o, bl), :] = at(st, o) * v - div_z(v, o)

    each_block(make_rw)
    to_y(T_RW, rw, rw_y)
    end_y(1, p1_y, T_P1, p1)

    start_y(rw_y, T_RW, 2, w_y)
    prepare_group()
    prepare_owners()

    arrived(T_P1, inner(p1))

    def rhs_u1(o):
        v = up(p1, o)
        ba[pl.ds(o + pad_x, bl), :] = at(src, o) - at(b0, o) + at(st, o) * v - div_z(v, o)

    each_block(rhs_u1)
    solve_x(u1)

    def make_b1(o):
        b1[pl.ds(o, bl), :] = at(src, o) - div_x(u1, o) - div_z(up(u1, o), o)

    each_block(make_b1)
    to_y(T_B1, b1, b1_y)

    middle_y(2)
    pick(3, p1[PAD : PAD + nx, :])
    start_y(b1_y, T_B1, 3, p2_y)
    end_y(2, w_y, T_W, w_x)

    arrived(T_W, inner(w_x))

    def make_late0(o):
        late0[pl.ds(o + PAD, bl), :] = up(w_x, o) - up(early1, o)

    each_block(make_late0)
    rhs_early(late0)
    solve_x(early0)
    middle_y(3)

    def make_sums(o):
        sum0[pl.ds(o + PAD, bl), :] = up(late0, o) + up(early0, o)
        both = up(late1, o) + up(early1, o)
        sum1[pl.ds(o + PAD, bl), :] = both
        grad_out[pl.ds(o, bl), :] = up(w_x, o) + up(early0, o) + up(late1, o)

    each_block(make_sums)

    def face_x(o):
        a = (up(sum0, o) - up(sum0, o, 1)) * (up(u0, o) - up(u0, o, 1))
        b = (up(sum1, o) - up(sum1, o, 1)) * (up(u1, o) - up(u1, o, 1))
        ba[pl.ds(o + pad_x, bl), :] = up(tx, o) * (a + b)

    each_block(face_x)

    def step_z(v):
        return v - next_layer(v)

    def cells_xz(o):
        z = step_z(up(early0, o)) * step_z(at(p0, o)) + step_z(up(late0, o)) * step_z(up(u0, o))
        z = z + step_z(up(early1, o)) * step_z(up(p1, o)) + step_z(up(late1, o)) * step_z(up(u1, o))
        z = at(tz, o) * z
        bb[pl.ds(o + pad_x, bl), :] = -0.5 * (big(ba, o) + big(ba, o, -1)) - 0.5 * (z + prev_layer(z))

    each_block(cells_xz)
    pick(7, bb[pad_x : pad_x + nx, :])
    pick(0, early0[PAD : PAD + nx, :])
    pick(2, w_x[PAD : PAD + nx, :])
    remote(msg_p, msg_r.at[1], T_MSG_P, prev_dev).start()
    remote(msg_n, msg_r.at[0], T_MSG_N, next_dev).start()
    arrived(T_TIN, tin_r)
    arrived(T_MSG_P, msg_r.at[1])
    arrived(T_MSG_N, msg_r.at[0])
    before = msg_r[0] - own_v[...]
    after = own_v[...] - msg_r[1]

    def pairs(d):
        return d[0:1] * d[1:2] + d[2:3] * d[3:4]

    own_line = own_v[7:8, :] - 0.5 * (own_v[6:7, :] * pairs(after) + msg_r[0, 6:7, :] * pairs(before))
    here = lax.broadcasted_iota(jnp.int32, (1, terms), 1) // cap == ni
    val_s[0] = jnp.where(here, jnp.concatenate([own_line[:, 0:cap]] * nn, axis=1), 0.0)

    end_y(3, p2_y)
    cells_y()
    val_s[0] = val_s[0] + pick_y()
    spread_narrow(T_VAL, lambda j: val_s.at[0], val_r.at[ni])
    arrived(T_VAL, val_r)

    totals = jnp.sum(val_r[...], axis=0)
    part_s[:, 0, :] = lax.dot_general(
        owner_hot[...] * jnp.broadcast_to(totals, (nw, terms)), place_hot[...],
        (((1,), (1,)), ((), ())), precision=HIGHEST, preferred_element_type=jnp.float32,
    )
    spread_wide(T_PART, part_s, part_r)
    arrived(T_PART, part_r)
    well_out[...] = jnp.sum(part_r[...], axis=0)

    for number in (T_TY, T_ST, T_SEED, T_B0, T_RW, T_B1, T_LATE1, T_P1, T_W):
        sent(number, ty_y.at[pl.ds(0, nn - 1)])
    sent(T_PNEXT, p_next)
    sent(T_FLUX, flux)
    sent(T_CELL_P, cell_s)
    sent(T_CELL_N, cell_s)
    sent(T_MSG_P, msg_p)
    sent(T_MSG_N, msg_n)
    sent(T_SLOT, slot_r.at[pl.ds(0, nn - 1)])
    sent(T_VAL, val_r.at[pl.ds(0, nn - 1)])
    sent(T_TIN, tin_s.at[pl.ds(0, nw - 1)])
    sent(T_COEF, coef_s.at[pl.ds(0, nw - 1)])
    for slot in range(4):
        sent(T_S0 + slot, to_s.at[slot, pl.ds(0, nw - 1)])
        sent(T_R0 + slot, re_s.at[slot, pl.ds(0, nw - 1)])
    sent(T_PART, part_s.at[pl.ds(0, nw - 1)])


def local(
    source, pressure_start, trans_x, trans_y, trans_z, storage, adjoint_seed,
    comp_cell, comp_well, comp_count, well_slot,
):
    _, nx, nk = source.shape
    nw, nn = lax.axis_size("wide"), lax.axis_size("narrow")
    cap = comp_cell.shape[1]
    owned = well_slot.shape[0] // (nw * nn)
    xc = nx // nn
    pad_w = max(PAD, nw // 2)
    f32 = jnp.float32

    def plain():
        return pltpu.VMEM((nx, nk), f32)

    def padded():
        return pltpu.VMEM((nx + 2 * PAD, nk), f32)

    def wide_pad():
        return pltpu.VMEM((2 * nx, nk), f32)

    def block():
        return pltpu.VMEM((nn, xc, nk), f32)

    def sep_pad():
        return pltpu.VMEM((nw + 2 * pad_w, nk), f32)

    def sep():
        return pltpu.VMEM((nw, nk), f32)

    def many(make, number):
        return [make() for _ in range(number)]

    scratch = (
        [plain(), plain(), padded()] + many(plain, 6)
        + many(block, 6) + many(block, 8)
        + many(padded, 3) + many(plain, 3) + many(padded, 7)
        + [pltpu.VMEM((levels_of(nx), nx, nk), f32)] * 2 + many(plain, 2) + many(wide_pad, 3)
        + [pltpu.VMEM((nw, 4, nk), f32)] * 2 + [pltpu.VMEM((4, nw, 2, nk), f32)] * 4
        + many(sep_pad, 3) + [pltpu.VMEM((levels_of(nw), nw, nk), f32)] * 2 + many(sep, 4)
        + [pltpu.VMEM((1, nk), f32), pltpu.VMEM((2, 1, nk), f32), pltpu.VMEM((8, nk), f32)]
        + [pltpu.VMEM((3 * cap, nx), f32), pltpu.VMEM((3 * cap, nk), f32), pltpu.VMEM((3 * cap, nk), f32)]
        + [pltpu.VMEM((8, nk), f32)] * 3 + [pltpu.VMEM((2, 8, nk), f32)]
        + [pltpu.VMEM((1, 2, nk), f32), pltpu.VMEM((nn, 2, nk), f32)]
        + [pltpu.VMEM((1, 1, nn * cap), f32), pltpu.VMEM((nn, 1, nn * cap), f32)]
        + [pltpu.VMEM((nw, 1, nk), f32)] * 4
        + [block(), pltpu.VMEM((nn, cap, xc), f32), pltpu.VMEM((nn, cap, nk), f32), pltpu.VMEM((nn * cap, nk), f32)]
        + [pltpu.VMEM((1, nn * cap), f32), pltpu.VMEM((nw, nn * cap), f32), pltpu.VMEM((nk, nn * cap), f32)]
        + [pltpu.SemaphoreType.DMA((T_COUNT,)), pltpu.SemaphoreType.DMA((T_COUNT,)), pltpu.SemaphoreType.DMA((L_COUNT,))]
    )
    hbm = pl.BlockSpec(memory_space=pl.ANY)
    vmem = pl.BlockSpec(memory_space=pltpu.VMEM)
    smem = pl.BlockSpec(memory_space=pltpu.SMEM)
    grad, sums = pl.pallas_call(
        functools.partial(kernel, nw, nn, nx, nk, cap, owned),
        out_shape=(jax.ShapeDtypeStruct((nx, nk), f32), jax.ShapeDtypeStruct((1, nk), f32)),
        in_specs=[hbm] * 7 + [vmem, vmem, smem, vmem],
        out_specs=(vmem, vmem),
        scratch_shapes=scratch,
        compiler_params=pltpu.CompilerParams(
            collective_id=0, has_side_effects=True, vmem_limit_bytes=62 * 1024 * 1024
        ),
    )(
        source[0], pressure_start[0], trans_x[0], trans_y[0], trans_z[0], storage[0], adjoint_seed[0],
        comp_cell, comp_well, comp_count.reshape(1, 1), well_slot.reshape(-1, nk),
    )
    return grad[None], sums[0, :owned]


def solution(mesh):
    cells = P(("wide", "narrow"), None, None)
    placed = (cells,) * 7 + (P(("wide", "narrow"), None), P(("wide", "narrow"), None), P(("wide", "narrow")), P())
    return jax.shard_map(
        local, mesh=mesh, in_specs=placed, out_specs=(cells, P(("wide", "narrow"))), check_vma=False
    )
```

```python
import functools

import jax
import jax.numpy as jnp
from jax import lax
from jax.experimental import pallas as pl
from jax.experimental.pallas import tpu as pltpu
from jax.sharding import PartitionSpec as P

MESH = pl.DeviceIdType.MESH
HIGHEST = lax.Precision.HIGHEST
PAD = 8

(
    T_TY, T_ST, T_SEED, T_B0, T_RW, T_B1, T_LATE1, T_P1, T_W, T_TIN,
    T_PNEXT, T_FLUX, T_CELL_P, T_CELL_N, T_SLOT, T_VAL, T_MSG_P, T_MSG_N,
    T_COEF, T_S0, T_S1, T_S2, T_S3, T_R0, T_R1, T_R2, T_R3, T_PART, T_COUNT,
) = range(29)
L_SRC, L_P0, L_TX, L_TY, L_TZ, L_ST, L_COUNT = range(7)


def levels_of(extent):
    return max(1, (extent - 1).bit_length())


def kernel(
    nw, nn, nx, nk, cap, owned,
    source, pressure, trans_x, trans_y, trans_z, storage, seed, cell, well, count, slots,
    grad_out, well_out,
    src, tx, tz, st, p_next, flux, f_prev,
    ty_y, st_y, seed_y, b0_y, rw_y, b1_y,
    inv_y, m_y, ga_y, gb_y, late1_y, p1_y, w_y, p2_y,
    late1, b0, b1, rw, u0, u1, early1, late0, sum0, sum1,
    gain_l, gain_r, inv_x, mid_x, ba, bb, bc,
    coef_s, coef_r, to_s, to_r, re_s, re_r,
    ia, ib, ic, pk_l, pk_r, pk_inv, tau, kap, f0s,
    cell_s, cell_r, pick_rows, onehot, lane_mask, gathered, own_v, msg_p, msg_n, msg_r,
    slot_s, slot_r, val_s, val_r, part_s, part_r,
    tin_s, tin_r, c_y, hot_y, mask_y, picked_y, slot_line, owner_hot, place_hot,
    fields, send_sem, recv_sem, load_sem,
):
    p0, ty = fields.at[0, pl.ds(PAD, nx)], fields.at[2, pl.ds(PAD, nx)]
    p1, early0, w_x = fields.at[1], fields.at[3], fields.at[4]
    wi, ni = lax.axis_index("wide"), lax.axis_index("narrow")
    rows = nw * nn
    row = wi * nn + ni
    nxt, prv = lax.rem(row + 1, rows), lax.rem(row + rows - 1, rows)
    next_dev = {"wide": nxt // nn, "narrow": lax.rem(nxt, nn)}
    prev_dev = {"wide": prv // nn, "narrow": lax.rem(prv, nn)}
    xc = nx // nn
    lev, pad_x = levels_of(nx), nx // 2
    lev_w, pad_w = levels_of(nw), max(PAD, nw // 2)
    bl = min(512, nx)
    blocks = nx // bl

    barrier = pltpu.get_barrier_semaphore()

    def greet_narrow(k, c):
        pl.semaphore_signal(barrier, inc=1, device_id={"narrow": lax.rem(ni + k, nn)}, device_id_type=MESH)
        return c

    def greet_wide(k, c):
        pl.semaphore_signal(barrier, inc=1, device_id={"wide": lax.rem(wi + k, nw)}, device_id_type=MESH)
        return c

    pl.semaphore_signal(barrier, inc=1, device_id=next_dev, device_id_type=MESH)
    pl.semaphore_signal(barrier, inc=1, device_id=prev_dev, device_id_type=MESH)
    lax.fori_loop(1, nn, greet_narrow, 0)
    lax.fori_loop(1, nw, greet_wide, 0)

    loads = [
        pltpu.make_async_copy(storage, st, load_sem.at[L_ST]),
        pltpu.make_async_copy(trans_x, tx.at[pl.ds(PAD, nx)], load_sem.at[L_TX]),
        pltpu.make_async_copy(trans_y, ty, load_sem.at[L_TY]),
        pltpu.make_async_copy(pressure, p0, load_sem.at[L_P0]),
        pltpu.make_async_copy(source, src, load_sem.at[L_SRC]),
        pltpu.make_async_copy(trans_z, tz, load_sem.at[L_TZ]),
    ]
    for one in loads:
        one.start()

    def remote(from_ref, to_ref, number, device):
        return pltpu.make_async_remote_copy(
            src_ref=from_ref, dst_ref=to_ref, send_sem=send_sem.at[number], recv_sem=recv_sem.at[number],
            device_id=device, device_id_type=MESH,
        )

    def spread_narrow(number, from_of, to_ref):
        def body(k, c):
            j = lax.rem(ni + k, nn)
            remote(from_of(j), to_ref, number, {"narrow": j}).start()
            return c

        lax.fori_loop(1, nn, body, 0)
        pltpu.make_async_copy(from_of(ni), to_ref, recv_sem.at[number]).start()

    def spread_wide(number, from_ref, to_ref):
        def body(k, c):
            j = lax.rem(wi + k, nw)
            remote(from_ref.at[j], to_ref.at[wi], number, {"wide": j}).start()
            return c

        lax.fori_loop(1, nw, body, 0)
        pltpu.make_async_copy(from_ref.at[wi], to_ref.at[wi], recv_sem.at[number]).start()

    def chunk(ref):
        return lambda j: ref.at[pl.ds(pl.multiple_of(j * xc, xc), xc)]

    def to_y(number, from_ref, to_ref):
        spread_narrow(number, chunk(from_ref), to_ref.at[ni])

    def to_x(number, from_ref, to_ref):
        spread_narrow(number, lambda j: from_ref.at[j], to_ref.at[pl.ds(pl.multiple_of(PAD + ni * xc, PAD), xc)])

    def arrived(number, ref):
        pltpu.make_async_copy(ref, ref, recv_sem.at[number]).wait()

    def sent(number, ref):
        pltpu.make_async_copy(ref, ref, send_sem.at[number]).wait()

    def inner(ref):
        return ref.at[pl.ds(PAD, nx)]

    zeros_pad = jnp.zeros((PAD, nk), jnp.float32)
    for ref in (tx, late1, p1, w_x, u0, u1, early1, early0, late0, sum0, sum1):
        ref[0:PAD, :] = zeros_pad
        ref[PAD + nx : 2 * PAD + nx, :] = zeros_pad
    zeros_x = jnp.zeros((pad_x, nk), jnp.float32)
    for ref in (ba, bb, bc):
        ref[0:pad_x, :] = zeros_x
        ref[pad_x + nx : 2 * pad_x + nx, :] = zeros_x
    zeros_w = jnp.zeros((pad_w, nk), jnp.float32)
    for ref in (ia, ib, ic):
        ref[0:pad_w, :] = zeros_w
        ref[pad_w + nw : 2 * pad_w + nw, :] = zeros_w
    for ref in (own_v, msg_p, msg_n):
        ref[...] = jnp.zeros_like(ref)

    cell_s[...] = jnp.zeros_like(cell_s)
    cell_s[0:1, 0:cap] = cell[...].astype(jnp.float32)

    def column(line):
        eye = lax.broadcasted_iota(jnp.int32, (cap, nk), 0) == lax.broadcasted_iota(jnp.int32, (cap, nk), 1)
        return jnp.sum(jnp.where(eye, jnp.broadcast_to(line, (cap, nk)), 0.0), axis=1, keepdims=True)

    def lanes_to_line(values):
        ones = jnp.ones((8, nk), jnp.float32)
        return lax.dot_general(
            ones, values, (((1,), (1,)), ((), ())), precision=HIGHEST, preferred_element_type=jnp.float32
        )[0:1, :]

    pick_rows[...] = jnp.zeros_like(pick_rows)
    pick_rows[0:1, 0:cap] = well[...].astype(jnp.float32)
    well_col = column(pick_rows[0:1, :])
    slot_rows = slots.shape[0]
    high = jnp.floor(well_col * (1.0 / nk))
    low = well_col - high * nk
    table_hot = jnp.where(
        jnp.broadcast_to(high, (cap, slot_rows)) == lax.broadcasted_iota(jnp.int32, (cap, slot_rows), 1).astype(jnp.float32),
        1.0, 0.0,
    )
    table = jnp.dot(table_hot, slots[...].astype(jnp.float32), precision=HIGHEST, preferred_element_type=jnp.float32)
    table = jnp.where(
        jnp.broadcast_to(low, (cap, nk)) == lax.broadcasted_iota(jnp.int32, (cap, nk), 1).astype(jnp.float32), table, 0.0
    )
    live = lax.broadcasted_iota(jnp.int32, (1, cap), 1) < count[0, 0]
    slot_s[...] = jnp.full_like(slot_s, -1.0)
    slot_s[0, 0:1, 0:cap] = jnp.where(live, lanes_to_line(table), -1.0)
    slot_s[0, 1:2, 0:cap] = cell_s[0:1, 0:cap]

    pl.semaphore_wait(barrier, nn - 1 + nw - 1 + 2)

    to_y(T_TY, trans_y, ty_y)
    to_y(T_ST, storage, st_y)
    remote(pressure, p_next, T_PNEXT, prev_dev).start()
    to_y(T_SEED, seed, seed_y)
    remote(cell_s, cell_r.at[1], T_CELL_P, prev_dev).start()
    remote(cell_s, cell_r.at[0], T_CELL_N, next_dev).start()
    spread_narrow(T_SLOT, lambda j: slot_s.at[0], slot_r.at[ni])

    def each_block(body):
        def step(i, c):
            body(pl.multiple_of(i * bl, bl))
            return c

        lax.fori_loop(0, blocks, step, 0)

    def at(ref, o, shift=0):
        return ref[pl.ds(o + shift, bl), :]

    def up(ref, o, shift=0):
        return ref[pl.ds(o + (PAD + shift), bl), :]

    def big(ref, o, shift=0):
        return ref[pl.ds(o + (pad_x + shift), bl), :]

    def next_layer(v):
        return pltpu.roll(v, nk - 1, 1)

    def prev_layer(v):
        return pltpu.roll(v, 1, 1)

    def div_z(v, o):
        f = at(tz, o) * (v - next_layer(v))
        return f - prev_layer(f)

    def div_x(ref, o):
        v = up(ref, o)
        return up(tx, o) * (v - up(ref, o, 1)) - up(tx, o, -1) * (up(ref, o, -1) - v)

    def solve_x(out):
        pair = (ba, bb)
        for level in range(lev):
            stride = 1 << level
            a, b = pair[level % 2], pair[1 - level % 2]

            def body(o):
                v = big(a, o)
                v = v + gain_l[level, pl.ds(o, bl), :] * big(a, o, -stride)
                v = v + gain_r[level, pl.ds(o, bl), :] * big(a, o, stride)
                if level == lev - 1:
                    out[pl.ds(o + PAD, bl), :] = v * at(inv_x, o)
                else:
                    b[pl.ds(o + pad_x, bl), :] = v

            each_block(body)

    def factor_x():
        def begin(o):
            t = up(tx, o)
            bb[pl.ds(o + pad_x, bl), :] = -t
            mid_x[pl.ds(o, bl), :] = at(st, o) + t + up(tx, o, -1)

        each_block(begin)
        pair = (bb, bc)
        for level in range(lev):
            stride = 1 << level
            a, b = pair[level % 2], pair[1 - level % 2]

            def invert(o):
                ba[pl.ds(o + pad_x, bl), :] = 1.0 / at(mid_x, o)

            def body(o):
                ua, ul = big(a, o), big(a, o, -stride)
                left = ul * big(ba, o, -stride)
                right = ua * big(ba, o, stride)
                gain_l[level, pl.ds(o, bl), :] = -left
                gain_r[level, pl.ds(o, bl), :] = -right
                b[pl.ds(o + pad_x, bl), :] = -right * big(a, o, stride)
                mid_x[pl.ds(o, bl), :] = at(mid_x, o) - left * ul - right * ua

            each_block(invert)
            each_block(body)

        def finish(o):
            inv_x[pl.ds(o, bl), :] = 1.0 / at(mid_x, o)

        each_block(finish)

    last = nn - 1

    def factor_y():
        def down(j, carry):
            delta, e = carry
            t = ty_y[j]
            iv = 1.0 / (delta + t)
            m = t * iv
            inv_y[j] = iv
            m_y[j] = m
            ga_y[j] = e
            return st_y[j + 1] + m * delta, m * e

        dee, kappa = lax.fori_loop(0, last, down, (st_y[0], jnp.ones((xc, nk), jnp.float32)))

        def back(i, carry):
            a, b = carry
            j = last - 1 - i
            m = m_y[j]
            a = inv_y[j] * ga_y[j] + m * a
            b = m * b
            ga_y[j] = a
            gb_y[j] = b
            return a, b

        corner, _ = lax.fori_loop(
            0, last, back, (jnp.zeros((xc, nk), jnp.float32), jnp.ones((xc, nk), jnp.float32))
        )
        t_last = jnp.where(wi == nw - 1, 0.0, ty_y[last])
        for number, value in enumerate((dee, kappa, corner, t_last)):
            coef_s[:, number, :] = value

    def reduce_y(rhs, slot):
        def body(j, carry):
            a, f = carry
            v = rhs[j]
            return a + gb_y[j] * v, f + ga_y[j] * v

        a, f = lax.fori_loop(0, last, body, (rhs[last], jnp.zeros((xc, nk), jnp.float32)), unroll=True)
        to_s[slot, :, 0, :] = a
        to_s[slot, :, 1, :] = f

    def inside_y(rhs, out):
        def down(j, c):
            out[j] = c
            return rhs[j + 1] + m_y[j] * c

        lax.fori_loop(0, last, down, rhs[0])

        def back(i, c):
            j = last - 1 - i
            c = inv_y[j] * out[j] + m_y[j] * c
            out[j] = c
            return c

        lax.fori_loop(0, last, back, jnp.zeros((xc, nk), jnp.float32))

    def complete_y(out, slot):
        phi = re_r[slot, :, 0, :]
        sep = re_r[slot, :, 1, :]

        def body(j, c):
            out[j] = out[j] + ga_y[j] * phi + gb_y[j] * sep
            return c

        lax.fori_loop(0, last, body, 0, unroll=True)
        out[last] = sep

    def mid(ref, shift=0):
        return ref[pad_w + shift : pad_w + shift + nw, :]

    def put(ref, value):
        ref[pad_w : pad_w + nw, :] = value

    def factor_sep():
        dee, kappa, corner, t_last = (coef_r[:, number, :] for number in range(4))
        put(ia, t_last)
        t_in = mid(ia, -1)
        tau_v = t_in / (1.0 + t_in * corner)
        tau[...] = tau_v
        kap[...] = kappa
        tin_s[:, 0, :] = t_in
        put(ia, tau_v)
        put(ib, tau_v * kappa)
        middle = dee + mid(ia, 1) + kappa * kappa * tau_v
        upper = -mid(ib, 1)
        for level in range(lev_w):
            stride = 1 << level
            put(ia, 1.0 / middle)
            put(ib, upper)
            lower = mid(ib, -stride)
            left = lower * mid(ia, -stride)
            right = upper * mid(ia, stride)
            pk_l[level] = -left
            pk_r[level] = -right
            middle = middle - left * lower - right * upper
            upper = -right * mid(ib, stride)
        pk_inv[...] = 1.0 / middle

    def solve_sep(slot):
        alpha = to_r[slot, :, 0, :]
        f0 = to_r[slot, :, 1, :]
        tf = tau[...] * f0
        put(ic, tf)
        v = alpha + mid(ic, 1) - kap[...] * tf
        for level in range(lev_w):
            stride = 1 << level
            ref = (ia, ib)[level % 2]
            put(ref, v)
            v = v + pk_l[level] * mid(ref, -stride) + pk_r[level] * mid(ref, stride)
        v = v * pk_inv[...]
        put(ic, v)
        re_s[slot, :, 0, :] = tau[...] * (mid(ic, -1) - f0 - kap[...] * v)
        re_s[slot, :, 1, :] = v

    def prepare_picks():
        for number, line in enumerate((cell_s[0:1, :], cell_r[0], cell_r[1])):
            col = column(line)
            x_of = jnp.floor(col * (1.0 / nk))
            layer = col - x_of * nk
            rows_at = pl.ds(number * cap, cap)
            onehot[rows_at, :] = jnp.where(
                jnp.broadcast_to(x_of, (cap, nx)) == lax.broadcasted_iota(jnp.int32, (cap, nx), 1).astype(jnp.float32), 1.0, 0.0
            )
            lane_mask[rows_at, :] = jnp.where(
                jnp.broadcast_to(layer, (cap, nk)) == lax.broadcasted_iota(jnp.int32, (cap, nk), 1).astype(jnp.float32), 1.0, 0.0
            )

    def pick_three(first):
        def body(i, c):
            number = first + i
            gathered[...] = lane_mask[...] * jnp.dot(
                onehot[...], fields[number, pl.ds(PAD, nx), :], precision=HIGHEST, preferred_element_type=jnp.float32
            )
            own_v[pl.ds(number, 1), 0:cap] = lanes_to_line(gathered[0:cap, :])
            msg_p[pl.ds(number, 1), 0:cap] = lanes_to_line(gathered[cap : 2 * cap, :])
            msg_n[pl.ds(number, 1), 0:cap] = lanes_to_line(gathered[2 * cap : 3 * cap, :])
            return c

        lax.fori_loop(0, 3, body, 0)

    terms = nn * cap

    def prepare_group():
        arrived(T_SLOT, slot_r)
        for j in range(nn):
            slot_line[0:1, j * cap : (j + 1) * cap] = slot_r[j, 0:1, 0:cap]

        def body(j, c):
            col = column(slot_r[j, 1:2, :])
            x_of = jnp.floor(col * (1.0 / nk))
            layer = col - x_of * nk
            x_of = x_of - (ni * xc).astype(jnp.float32)
            hot_y[j] = jnp.where(
                jnp.broadcast_to(x_of, (cap, xc)) == lax.broadcasted_iota(jnp.int32, (cap, xc), 1).astype(jnp.float32), 1.0, 0.0
            )
            mask_y[j] = jnp.where(
                jnp.broadcast_to(layer, (cap, nk)) == lax.broadcasted_iota(jnp.int32, (cap, nk), 1).astype(jnp.float32), 1.0, 0.0
            )
            return c

        lax.fori_loop(0, nn, body, 0)

    def prepare_owners():
        s_line = slot_line[...]
        base = ((lax.broadcasted_iota(jnp.int32, (nw, terms), 0) * nn + ni) * owned).astype(jnp.float32)
        s_all = jnp.broadcast_to(s_line, (nw, terms))
        owner_hot[...] = jnp.where((s_all >= base) & (s_all < base + owned), 1.0, 0.0)
        rest = s_line - owned * jnp.floor((s_line + 0.5) * (1.0 / owned))
        place_hot[...] = jnp.where(
            jnp.broadcast_to(rest, (nk, terms)) == lax.broadcasted_iota(jnp.int32, (nk, terms), 0).astype(jnp.float32), 1.0, 0.0
        )

    def cells_y():
        t_in = tin_r[:, 0, :]
        there = t_in > 0.0
        e0 = jnp.where(there, re_r[0, :, 0, :] * re_r[3, :, 0, :] / jnp.where(there, t_in, 1.0), 0.0)

        def body(j, before):
            e = ty_y[j] * (late1_y[j] - late1_y[j + 1]) * (p2_y[j] - p2_y[j + 1])
            c_y[j] = -0.5 * (e + before)
            return e

        before = lax.fori_loop(0, last, body, e0)

        def out_flux(rhs, v):
            return rhs[last] - st_y[last] * v[last] - ty_y[last - 1] * (v[last] - v[last - 1])

        e = jnp.where(wi == nw - 1, 0.0, out_flux(seed_y, late1_y) * out_flux(b1_y, p2_y) / ty_y[last])
        c_y[last] = -0.5 * (e + before)

    def pick_y():
        for j in range(nn):
            picked_y[j * cap : (j + 1) * cap, :] = mask_y[j] * jnp.dot(
                hot_y[j], c_y[j], precision=HIGHEST, preferred_element_type=jnp.float32
            )
        return lanes_to_line(picked_y[...])

    def start_y(rhs, number, slot, out):
        arrived(number, rhs)
        reduce_y(rhs, slot)
        spread_wide(T_S0 + slot, to_s.at[slot], to_r.at[slot])
        inside_y(rhs, out)

    def middle_y(slot):
        arrived(T_S0 + slot, to_r.at[slot])
        solve_sep(slot)
        spread_wide(T_R0 + slot, re_s.at[slot], re_r.at[slot])

    def end_y(slot, out, number=None, to_ref=None):
        arrived(T_R0 + slot, re_r.at[slot])
        complete_y(out, slot)
        if number is not None:
            to_x(number, out, to_ref)

    loads[0].wait()
    loads[1].wait()
    tx[PAD + nx - 1 : PAD + nx, :] = jnp.zeros((1, nk), jnp.float32)
    factor_x()
    for one in loads[2:]:
        one.wait()
    lane = lax.broadcasted_iota(jnp.int32, (bl, nk), 1)
    open_y = row < rows - 1

    arrived(T_TY, ty_y)
    arrived(T_ST, st_y)
    factor_y()
    spread_wide(T_COEF, coef_s, coef_r)

    arrived(T_PNEXT, p_next)

    def make_flux(o):
        tz[pl.ds(o, bl), :] = jnp.where(lane < nk - 1, at(tz, o), 0.0)
        t = jnp.where(open_y, at(ty, o), 0.0)
        ty[pl.ds(o, bl), :] = t
        flux[pl.ds(o, bl), :] = t * (at(p0, o) - at(p_next, o))

    each_block(make_flux)
    remote(flux, f_prev, T_FLUX, next_dev).start()

    start_y(seed_y, T_SEED, 0, late1_y)

    arrived(T_CELL_P, cell_r.at[1])
    arrived(T_CELL_N, cell_r.at[0])
    prepare_picks()

    arrived(T_FLUX, f_prev)

    def rhs_u0(o):
        ba[pl.ds(o + pad_x, bl), :] = at(src, o) - (at(flux, o) - at(f_prev, o)) - div_z(at(p0, o), o)

    each_block(rhs_u0)
    solve_x(u0)

    def make_b0(o):
        b0[pl.ds(o, bl), :] = at(src, o) - div_x(u0, o) - div_z(up(u0, o), o)

    each_block(make_b0)
    to_y(T_B0, b0, b0_y)

    arrived(T_COEF, coef_r)
    factor_sep()
    middle_y(0)

    start_y(b0_y, T_B0, 1, p1_y)
    end_y(0, late1_y, T_LATE1, late1)
    middle_y(1)

    arrived(T_LATE1, inner(late1))

    def rhs_early(ref):
        def body(o):
            ba[pl.ds(o + pad_x, bl), :] = -(div_x(ref, o) + div_z(up(ref, o), o))

        each_block(body)

    rhs_early(late1)
    solve_x(early1)

    def make_rw(o):
        v = up(early1, o)
        rw[pl.ds(o, bl), :] = at(st, o) * v - div_z(v, o)

    each_block(make_rw)
    to_y(T_RW, rw, rw_y)
    end_y(1, p1_y, T_P1, p1)
    spread_wide(T_TIN, tin_s, tin_r)

    start_y(rw_y, T_RW, 2, w_y)
    prepare_group()
    prepare_owners()

    arrived(T_P1, inner(p1))

    def rhs_u1(o):
        v = up(p1, o)
        ba[pl.ds(o + pad_x, bl), :] = at(src, o) - at(b0, o) + at(st, o) * v - div_z(v, o)

    each_block(rhs_u1)
    solve_x(u1)

    def make_b1(o):
        b1[pl.ds(o, bl), :] = at(src, o) - div_x(u1, o) - div_z(up(u1, o), o)

    each_block(make_b1)
    to_y(T_B1, b1, b1_y)

    middle_y(2)
    pick_three(0)
    start_y(b1_y, T_B1, 3, p2_y)
    end_y(2, w_y, T_W, w_x)

    arrived(T_W, inner(w_x))

    def make_late0(o):
        late0[pl.ds(o + PAD, bl), :] = up(w_x, o) - up(early1, o)

    each_block(make_late0)
    rhs_early(late0)
    solve_x(early0)
    middle_y(3)

    def make_sums(o):
        sum0[pl.ds(o + PAD, bl), :] = up(late0, o) + up(early0, o)
        both = up(late1, o) + up(early1, o)
        sum1[pl.ds(o + PAD, bl), :] = both
        grad_out[pl.ds(o, bl), :] = up(w_x, o) + up(early0, o) + up(late1, o)

    each_block(make_sums)

    def face_x(o):
        a = (up(sum0, o) - up(sum0, o, 1)) * (up(u0, o) - up(u0, o, 1))
        b = (up(sum1, o) - up(sum1, o, 1)) * (up(u1, o) - up(u1, o, 1))
        ba[pl.ds(o + pad_x, bl), :] = up(tx, o) * (a + b)

    each_block(face_x)

    def step_z(v):
        return v - next_layer(v)

    def cells_xz(o):
        z = step_z(up(early0, o)) * step_z(at(p0, o)) + step_z(up(late0, o)) * step_z(up(u0, o))
        z = z + step_z(up(early1, o)) * step_z(up(p1, o)) + step_z(up(late1, o)) * step_z(up(u1, o))
        z = at(tz, o) * z
        fields[5, pl.ds(o + PAD, bl), :] = -0.5 * (big(ba, o) + big(ba, o, -1)) - 0.5 * (z + prev_layer(z))

    each_block(cells_xz)
    pick_three(3)
    remote(msg_p, msg_r.at[1], T_MSG_P, prev_dev).start()
    remote(msg_n, msg_r.at[0], T_MSG_N, next_dev).start()
    arrived(T_TIN, tin_r)

    end_y(3, p2_y)
    cells_y()
    from_block = pick_y()

    arrived(T_MSG_P, msg_r.at[1])
    arrived(T_MSG_N, msg_r.at[0])
    before = msg_r[0] - own_v[...]
    after = own_v[...] - msg_r[1]

    def pairs(d):
        return d[3:4] * d[0:1] + d[4:5] * d[1:2]

    own_line = own_v[5:6, :] - 0.5 * (own_v[2:3, :] * pairs(after) + msg_r[0, 2:3, :] * pairs(before))
    here = lax.broadcasted_iota(jnp.int32, (1, terms), 1) // cap == ni
    val_s[0] = from_block + jnp.where(here, jnp.concatenate([own_line[:, 0:cap]] * nn, axis=1), 0.0)
    spread_narrow(T_VAL, lambda j: val_s.at[0], val_r.at[ni])
    arrived(T_VAL, val_r)

    totals = jnp.sum(val_r[...], axis=0)
    part_s[:, 0, :] = lax.dot_general(
        owner_hot[...] * jnp.broadcast_to(totals, (nw, terms)), place_hot[...],
        (((1,), (1,)), ((), ())), precision=HIGHEST, preferred_element_type=jnp.float32,
    )
    spread_wide(T_PART, part_s, part_r)
    arrived(T_PART, part_r)
    well_out[...] = jnp.sum(part_r[...], axis=0)

    for number in (T_TY, T_ST, T_SEED, T_B0, T_RW, T_B1, T_LATE1, T_P1, T_W):
        sent(number, ty_y.at[pl.ds(0, nn - 1)])
    sent(T_PNEXT, p_next)
    sent(T_FLUX, flux)
    sent(T_CELL_P, cell_s)
    sent(T_CELL_N, cell_s)
    sent(T_MSG_P, msg_p)
    sent(T_MSG_N, msg_n)
    sent(T_SLOT, slot_r.at[pl.ds(0, nn - 1)])
    sent(T_VAL, val_r.at[pl.ds(0, nn - 1)])
    sent(T_TIN, tin_s.at[pl.ds(0, nw - 1)])
    sent(T_COEF, coef_s.at[pl.ds(0, nw - 1)])
    for slot in range(4):
        sent(T_S0 + slot, to_s.at[slot, pl.ds(0, nw - 1)])
        sent(T_R0 + slot, re_s.at[slot, pl.ds(0, nw - 1)])
    sent(T_PART, part_s.at[pl.ds(0, nw - 1)])


def local(
    source, pressure_start, trans_x, trans_y, trans_z, storage, adjoint_seed,
    comp_cell, comp_well, comp_count, well_slot,
):
    _, nx, nk = source.shape
    nw, nn = lax.axis_size("wide"), lax.axis_size("narrow")
    cap = comp_cell.shape[1]
    owned = well_slot.shape[0] // (nw * nn)
    xc = nx // nn
    pad_w = max(PAD, nw // 2)
    f32 = jnp.float32

    def plain():
        return pltpu.VMEM((nx, nk), f32)

    def padded():
        return pltpu.VMEM((nx + 2 * PAD, nk), f32)

    def wide_pad():
        return pltpu.VMEM((2 * nx, nk), f32)

    def block():
        return pltpu.VMEM((nn, xc, nk), f32)

    def sep_pad():
        return pltpu.VMEM((nw + 2 * pad_w, nk), f32)

    def sep():
        return pltpu.VMEM((nw, nk), f32)

    def many(make, number):
        return [make() for _ in range(number)]

    scratch = (
        [plain(), padded()] + many(plain, 5)
        + many(block, 6) + many(block, 8)
        + many(padded, 1) + many(plain, 3) + many(padded, 6)
        + [pltpu.VMEM((levels_of(nx), nx, nk), f32)] * 2 + many(plain, 2) + many(wide_pad, 3)
        + [pltpu.VMEM((nw, 4, nk), f32)] * 2 + [pltpu.VMEM((4, nw, 2, nk), f32)] * 4
        + many(sep_pad, 3) + [pltpu.VMEM((levels_of(nw), nw, nk), f32)] * 2 + many(sep, 4)
        + [pltpu.VMEM((1, nk), f32), pltpu.VMEM((2, 1, nk), f32), pltpu.VMEM((8, nk), f32)]
        + [pltpu.VMEM((3 * cap, nx), f32), pltpu.VMEM((3 * cap, nk), f32), pltpu.VMEM((3 * cap, nk), f32)]
        + [pltpu.VMEM((8, nk), f32)] * 3 + [pltpu.VMEM((2, 8, nk), f32)]
        + [pltpu.VMEM((1, 2, nk), f32), pltpu.VMEM((nn, 2, nk), f32)]
        + [pltpu.VMEM((1, 1, nn * cap), f32), pltpu.VMEM((nn, 1, nn * cap), f32)]
        + [pltpu.VMEM((nw, 1, nk), f32)] * 4
        + [block(), pltpu.VMEM((nn, cap, xc), f32), pltpu.VMEM((nn, cap, nk), f32), pltpu.VMEM((nn * cap, nk), f32)]
        + [pltpu.VMEM((1, nn * cap), f32), pltpu.VMEM((nw, nn * cap), f32), pltpu.VMEM((nk, nn * cap), f32)]
        + [pltpu.VMEM((6, nx + 2 * PAD, nk), f32)]
        + [pltpu.SemaphoreType.DMA((T_COUNT,)), pltpu.SemaphoreType.DMA((T_COUNT,)), pltpu.SemaphoreType.DMA((L_COUNT,))]
    )
    hbm = pl.BlockSpec(memory_space=pl.ANY)
    vmem = pl.BlockSpec(memory_space=pltpu.VMEM)
    smem = pl.BlockSpec(memory_space=pltpu.SMEM)
    grad, sums = pl.pallas_call(
        functools.partial(kernel, nw, nn, nx, nk, cap, owned),
        out_shape=(jax.ShapeDtypeStruct((nx, nk), f32), jax.ShapeDtypeStruct((1, nk), f32)),
        in_specs=[hbm] * 7 + [vmem, vmem, smem, vmem],
        out_specs=(vmem, vmem),
        scratch_shapes=scratch,
        compiler_params=pltpu.CompilerParams(
            collective_id=0, has_side_effects=True, vmem_limit_bytes=62 * 1024 * 1024
        ),
    )(
        source[0], pressure_start[0], trans_x[0], trans_y[0], trans_z[0], storage[0], adjoint_seed[0],
        comp_cell, comp_well, comp_count.reshape(1, 1), well_slot.reshape(-1, nk),
    )
    return grad[None], sums[0, :owned]


def solution(mesh):
    cells = P(("wide", "narrow"), None, None)
    placed = (cells,) * 7 + (P(("wide", "narrow"), None), P(("wide", "narrow"), None), P(("wide", "narrow")), P())
    return jax.shard_map(
        local, mesh=mesh, in_specs=placed, out_specs=(cells, P(("wide", "narrow"))), check_vma=False
    )
```

```python
import functools

import jax
import jax.numpy as jnp
from jax import lax
from jax.experimental import pallas as pl
from jax.experimental.pallas import tpu as pltpu
from jax.sharding import PartitionSpec as P

MESH = pl.DeviceIdType.MESH
HIGHEST = lax.Precision.HIGHEST
PAD = 8

(
    T_TY, T_ST, T_SEED, T_B0, T_RW, T_B1, T_LATE1, T_P1, T_W, T_TIN,
    T_PNEXT, T_FLUX, T_CELL_P, T_CELL_N, T_SLOT, T_VAL, T_MSG_P, T_MSG_N,
    T_COEF, T_S0, T_S1, T_S2, T_S3, T_R0, T_R1, T_R2, T_R3, T_PART, T_PIECE, T_COUNT_BASE,
) = range(30)
PIECES = 4
T_COUNT = T_PIECE + 2 * PIECES
L_SRC, L_P0, L_TX, L_TY, L_TZ, L_ST, L_COUNT = range(7)


def levels_of(extent):
    return max(1, (extent - 1).bit_length())


def kernel(
    nw, nn, nx, nk, cap, owned,
    source, pressure, trans_x, trans_y, trans_z, storage, seed, cell, well, count, slots,
    grad_out, well_out,
    src, tx, tz, st, p_next, flux, f_prev,
    ty_y, st_y, seed_y, b0_y, rw_y, b1_y,
    inv_y, m_y, ga_y, gb_y, late1_y, p1_y, w_y, p2_y,
    late1, b0, b1, rw, u0, u1, early1, late0, sum0, sum1,
    gain_l, gain_r, inv_x, mid_x, ba, bb, bc,
    coef_s, coef_r, to_s, to_r, re_s, re_r,
    ia, ib, ic, pk_l, pk_r, pk_inv, tau, kap, f0s,
    cell_s, cell_r, pick_rows, onehot, lane_mask, gathered, own_v, msg_p, msg_n, msg_r,
    slot_s, slot_r, val_s, val_r, part_s, part_r,
    tin_s, tin_r, c_y, hot_y, mask_y, picked_y, slot_line, owner_hot, place_hot,
    fields, send_sem, recv_sem, load_sem,
):
    p0, ty = fields.at[0, pl.ds(PAD, nx)], fields.at[2, pl.ds(PAD, nx)]
    p1, early0, w_x = fields.at[1], fields.at[3], fields.at[4]
    wi, ni = lax.axis_index("wide"), lax.axis_index("narrow")
    rows = nw * nn
    row = wi * nn + ni
    nxt, prv = lax.rem(row + 1, rows), lax.rem(row + rows - 1, rows)
    next_dev = {"wide": nxt // nn, "narrow": lax.rem(nxt, nn)}
    prev_dev = {"wide": prv // nn, "narrow": lax.rem(prv, nn)}
    xc = nx // nn
    lev, pad_x = levels_of(nx), nx // 2
    lev_w, pad_w = levels_of(nw), max(PAD, nw // 2)
    bl = min(512, nx)
    blocks = nx // bl

    barrier = pltpu.get_barrier_semaphore()

    def greet_narrow(k, c):
        pl.semaphore_signal(barrier, inc=1, device_id={"narrow": lax.rem(ni + k, nn)}, device_id_type=MESH)
        return c

    def greet_wide(k, c):
        pl.semaphore_signal(barrier, inc=1, device_id={"wide": lax.rem(wi + k, nw)}, device_id_type=MESH)
        return c

    pl.semaphore_signal(barrier, inc=1, device_id=next_dev, device_id_type=MESH)
    pl.semaphore_signal(barrier, inc=1, device_id=prev_dev, device_id_type=MESH)
    lax.fori_loop(1, nn, greet_narrow, 0)
    lax.fori_loop(1, nw, greet_wide, 0)

    loads = [
        pltpu.make_async_copy(storage, st, load_sem.at[L_ST]),
        pltpu.make_async_copy(trans_x, tx.at[pl.ds(PAD, nx)], load_sem.at[L_TX]),
        pltpu.make_async_copy(trans_y, ty, load_sem.at[L_TY]),
        pltpu.make_async_copy(pressure, p0, load_sem.at[L_P0]),
        pltpu.make_async_copy(source, src, load_sem.at[L_SRC]),
        pltpu.make_async_copy(trans_z, tz, load_sem.at[L_TZ]),
    ]
    for one in loads:
        one.start()

    def remote(from_ref, to_ref, number, device):
        return pltpu.make_async_remote_copy(
            src_ref=from_ref, dst_ref=to_ref, send_sem=send_sem.at[number], recv_sem=recv_sem.at[number],
            device_id=device, device_id_type=MESH,
        )

    def spread_narrow(number, from_of, to_ref):
        def body(k, c):
            j = lax.rem(ni + k, nn)
            remote(from_of(j), to_ref, number, {"narrow": j}).start()
            return c

        lax.fori_loop(1, nn, body, 0)
        pltpu.make_async_copy(from_of(ni), to_ref, recv_sem.at[number]).start()

    def spread_wide(number, from_ref, to_ref):
        def body(k, c):
            j = lax.rem(wi + k, nw)
            remote(from_ref.at[j], to_ref.at[wi], number, {"wide": j}).start()
            return c

        lax.fori_loop(1, nw, body, 0)
        pltpu.make_async_copy(from_ref.at[wi], to_ref.at[wi], recv_sem.at[number]).start()

    def chunk(ref):
        return lambda j: ref.at[pl.ds(pl.multiple_of(j * xc, xc), xc)]

    def to_y(number, from_ref, to_ref):
        spread_narrow(number, chunk(from_ref), to_ref.at[ni])

    def to_x(number, from_ref, to_ref):
        spread_narrow(number, lambda j: from_ref.at[j], to_ref.at[pl.ds(pl.multiple_of(PAD + ni * xc, PAD), xc)])

    def arrived(number, ref):
        pltpu.make_async_copy(ref, ref, recv_sem.at[number]).wait()

    def sent(number, ref):
        pltpu.make_async_copy(ref, ref, send_sem.at[number]).wait()

    def inner(ref):
        return ref.at[pl.ds(PAD, nx)]

    zeros_pad = jnp.zeros((PAD, nk), jnp.float32)
    for ref in (tx, late1, p1, w_x, u0, u1, early1, early0, late0, sum0, sum1):
        ref[0:PAD, :] = zeros_pad
        ref[PAD + nx : 2 * PAD + nx, :] = zeros_pad
    zeros_x = jnp.zeros((pad_x, nk), jnp.float32)
    for ref in (ba, bb, bc):
        ref[0:pad_x, :] = zeros_x
        ref[pad_x + nx : 2 * pad_x + nx, :] = zeros_x
    zeros_w = jnp.zeros((pad_w, nk), jnp.float32)
    for ref in (ia, ib, ic):
        ref[0:pad_w, :] = zeros_w
        ref[pad_w + nw : 2 * pad_w + nw, :] = zeros_w
    for ref in (own_v, msg_p, msg_n):
        ref[...] = jnp.zeros_like(ref)

    cell_s[...] = jnp.zeros_like(cell_s)
    cell_s[0:1, 0:cap] = cell[...].astype(jnp.float32)

    def column(line):
        eye = lax.broadcasted_iota(jnp.int32, (cap, nk), 0) == lax.broadcasted_iota(jnp.int32, (cap, nk), 1)
        return jnp.sum(jnp.where(eye, jnp.broadcast_to(line, (cap, nk)), 0.0), axis=1, keepdims=True)

    def lanes_to_line(values):
        ones = jnp.ones((8, nk), jnp.float32)
        return lax.dot_general(
            ones, values, (((1,), (1,)), ((), ())), precision=HIGHEST, preferred_element_type=jnp.float32
        )[0:1, :]

    pick_rows[...] = jnp.zeros_like(pick_rows)
    pick_rows[0:1, 0:cap] = well[...].astype(jnp.float32)
    well_col = column(pick_rows[0:1, :])
    slot_rows = slots.shape[0]
    high = jnp.floor(well_col * (1.0 / nk))
    low = well_col - high * nk
    table_hot = jnp.where(
        jnp.broadcast_to(high, (cap, slot_rows)) == lax.broadcasted_iota(jnp.int32, (cap, slot_rows), 1).astype(jnp.float32),
        1.0, 0.0,
    )
    table = jnp.dot(table_hot, slots[...].astype(jnp.float32), precision=HIGHEST, preferred_element_type=jnp.float32)
    table = jnp.where(
        jnp.broadcast_to(low, (cap, nk)) == lax.broadcasted_iota(jnp.int32, (cap, nk), 1).astype(jnp.float32), table, 0.0
    )
    live = lax.broadcasted_iota(jnp.int32, (1, cap), 1) < count[0, 0]
    slot_s[...] = jnp.full_like(slot_s, -1.0)
    slot_s[0, 0:1, 0:cap] = jnp.where(live, lanes_to_line(table), -1.0)
    slot_s[0, 1:2, 0:cap] = cell_s[0:1, 0:cap]

    pl.semaphore_wait(barrier, nn - 1 + nw - 1 + 2)

    to_y(T_TY, trans_y, ty_y)
    to_y(T_ST, storage, st_y)
    piece = nx // PIECES

    def part(ref, i):
        return ref.at[pl.ds(i * piece, piece)]

    for i in range(PIECES):
        remote(part(pressure, i), part(p_next, i), T_PIECE + i, prev_dev).start()
    to_y(T_SEED, seed, seed_y)
    remote(cell_s, cell_r.at[1], T_CELL_P, prev_dev).start()
    remote(cell_s, cell_r.at[0], T_CELL_N, next_dev).start()
    spread_narrow(T_SLOT, lambda j: slot_s.at[0], slot_r.at[ni])

    def each_block(body):
        def step(i, c):
            body(pl.multiple_of(i * bl, bl))
            return c

        lax.fori_loop(0, blocks, step, 0)

    def at(ref, o, shift=0):
        return ref[pl.ds(o + shift, bl), :]

    def up(ref, o, shift=0):
        return ref[pl.ds(o + (PAD + shift), bl), :]

    def big(ref, o, shift=0):
        return ref[pl.ds(o + (pad_x + shift), bl), :]

    def next_layer(v):
        return pltpu.roll(v, nk - 1, 1)

    def prev_layer(v):
        return pltpu.roll(v, 1, 1)

    def div_z(v, o):
        f = at(tz, o) * (v - next_layer(v))
        return f - prev_layer(f)

    def div_x(ref, o):
        v = up(ref, o)
        return up(tx, o) * (v - up(ref, o, 1)) - up(tx, o, -1) * (up(ref, o, -1) - v)

    def solve_x(out):
        pair = (ba, bb)
        for level in range(lev):
            stride = 1 << level
            a, b = pair[level % 2], pair[1 - level % 2]

            def body(o):
                v = big(a, o)
                v = v + gain_l[level, pl.ds(o, bl), :] * big(a, o, -stride)
                v = v + gain_r[level, pl.ds(o, bl), :] * big(a, o, stride)
                if level == lev - 1:
                    out[pl.ds(o + PAD, bl), :] = v * at(inv_x, o)
                else:
                    b[pl.ds(o + pad_x, bl), :] = v

            each_block(body)

    def factor_x():
        def begin(o):
            t = up(tx, o)
            bb[pl.ds(o + pad_x, bl), :] = -t
            mid_x[pl.ds(o, bl), :] = at(st, o) + t + up(tx, o, -1)

        each_block(begin)
        pair = (bb, bc)
        for level in range(lev):
            stride = 1 << level
            a, b = pair[level % 2], pair[1 - level % 2]

            def invert(o):
                ba[pl.ds(o + pad_x, bl), :] = 1.0 / at(mid_x, o)

            def body(o):
                ua, ul = big(a, o), big(a, o, -stride)
                left = ul * big(ba, o, -stride)
                right = ua * big(ba, o, stride)
                gain_l[level, pl.ds(o, bl), :] = -left
                gain_r[level, pl.ds(o, bl), :] = -right
                b[pl.ds(o + pad_x, bl), :] = -right * big(a, o, stride)
                mid_x[pl.ds(o, bl), :] = at(mid_x, o) - left * ul - right * ua

            each_block(invert)
            each_block(body)

        def finish(o):
            inv_x[pl.ds(o, bl), :] = 1.0 / at(mid_x, o)

        each_block(finish)

    last = nn - 1

    def factor_y():
        def down(j, carry):
            delta, e = carry
            t = ty_y[j]
            iv = 1.0 / (delta + t)
            m = t * iv
            inv_y[j] = iv
            m_y[j] = m
            ga_y[j] = e
            return st_y[j + 1] + m * delta, m * e

        dee, kappa = lax.fori_loop(0, last, down, (st_y[0], jnp.ones((xc, nk), jnp.float32)))

        def back(i, carry):
            a, b = carry
            j = last - 1 - i
            m = m_y[j]
            a = inv_y[j] * ga_y[j] + m * a
            b = m * b
            ga_y[j] = a
            gb_y[j] = b
            return a, b

        corner, _ = lax.fori_loop(
            0, last, back, (jnp.zeros((xc, nk), jnp.float32), jnp.ones((xc, nk), jnp.float32))
        )
        t_last = jnp.where(wi == nw - 1, 0.0, ty_y[last])
        for number, value in enumerate((dee, kappa, corner, t_last)):
            coef_s[:, number, :] = value

    def reduce_y(rhs, slot):
        def body(j, carry):
            a, f = carry
            v = rhs[j]
            return a + gb_y[j] * v, f + ga_y[j] * v

        a, f = lax.fori_loop(0, last, body, (rhs[last], jnp.zeros((xc, nk), jnp.float32)), unroll=True)
        to_s[slot, :, 0, :] = a
        to_s[slot, :, 1, :] = f

    def inside_y(rhs, out):
        def down(j, c):
            out[j] = c
            return rhs[j + 1] + m_y[j] * c

        lax.fori_loop(0, last, down, rhs[0])

        def back(i, c):
            j = last - 1 - i
            c = inv_y[j] * out[j] + m_y[j] * c
            out[j] = c
            return c

        lax.fori_loop(0, last, back, jnp.zeros((xc, nk), jnp.float32))

    def complete_y(out, slot):
        phi = re_r[slot, :, 0, :]
        sep = re_r[slot, :, 1, :]

        def body(j, c):
            out[j] = out[j] + ga_y[j] * phi + gb_y[j] * sep
            return c

        lax.fori_loop(0, last, body, 0, unroll=True)
        out[last] = sep

    def mid(ref, shift=0):
        return ref[pad_w + shift : pad_w + shift + nw, :]

    def put(ref, value):
        ref[pad_w : pad_w + nw, :] = value

    def factor_sep():
        dee, kappa, corner, t_last = (coef_r[:, number, :] for number in range(4))
        put(ia, t_last)
        t_in = mid(ia, -1)
        tau_v = t_in / (1.0 + t_in * corner)
        tau[...] = tau_v
        kap[...] = kappa
        tin_s[:, 0, :] = t_in
        put(ia, tau_v)
        put(ib, tau_v * kappa)
        middle = dee + mid(ia, 1) + kappa * kappa * tau_v
        upper = -mid(ib, 1)
        for level in range(lev_w):
            stride = 1 << level
            put(ia, 1.0 / middle)
            put(ib, upper)
            lower = mid(ib, -stride)
            left = lower * mid(ia, -stride)
            right = upper * mid(ia, stride)
            pk_l[level] = -left
            pk_r[level] = -right
            middle = middle - left * lower - right * upper
            upper = -right * mid(ib, stride)
        pk_inv[...] = 1.0 / middle

    def solve_sep(slot):
        alpha = to_r[slot, :, 0, :]
        f0 = to_r[slot, :, 1, :]
        tf = tau[...] * f0
        put(ic, tf)
        v = alpha + mid(ic, 1) - kap[...] * tf
        for level in range(lev_w):
            stride = 1 << level
            ref = (ia, ib)[level % 2]
            put(ref, v)
            v = v + pk_l[level] * mid(ref, -stride) + pk_r[level] * mid(ref, stride)
        v = v * pk_inv[...]
        put(ic, v)
        re_s[slot, :, 0, :] = tau[...] * (mid(ic, -1) - f0 - kap[...] * v)
        re_s[slot, :, 1, :] = v

    def prepare_picks():
        for number, line in enumerate((cell_s[0:1, :], cell_r[0], cell_r[1])):
            col = column(line)
            x_of = jnp.floor(col * (1.0 / nk))
            layer = col - x_of * nk
            rows_at = pl.ds(number * cap, cap)
            onehot[rows_at, :] = jnp.where(
                jnp.broadcast_to(x_of, (cap, nx)) == lax.broadcasted_iota(jnp.int32, (cap, nx), 1).astype(jnp.float32), 1.0, 0.0
            )
            lane_mask[rows_at, :] = jnp.where(
                jnp.broadcast_to(layer, (cap, nk)) == lax.broadcasted_iota(jnp.int32, (cap, nk), 1).astype(jnp.float32), 1.0, 0.0
            )

    def pick_three(first):
        def body(i, c):
            number = first + i
            gathered[...] = lane_mask[...] * jnp.dot(
                onehot[...], fields[number, pl.ds(PAD, nx), :], precision=HIGHEST, preferred_element_type=jnp.float32
            )
            own_v[pl.ds(number, 1), 0:cap] = lanes_to_line(gathered[0:cap, :])
            msg_p[pl.ds(number, 1), 0:cap] = lanes_to_line(gathered[cap : 2 * cap, :])
            msg_n[pl.ds(number, 1), 0:cap] = lanes_to_line(gathered[2 * cap : 3 * cap, :])
            return c

        lax.fori_loop(0, 3, body, 0)

    terms = nn * cap

    def prepare_group():
        arrived(T_SLOT, slot_r)
        for j in range(nn):
            slot_line[0:1, j * cap : (j + 1) * cap] = slot_r[j, 0:1, 0:cap]

        def body(j, c):
            col = column(slot_r[j, 1:2, :])
            x_of = jnp.floor(col * (1.0 / nk))
            layer = col - x_of * nk
            x_of = x_of - (ni * xc).astype(jnp.float32)
            hot_y[j] = jnp.where(
                jnp.broadcast_to(x_of, (cap, xc)) == lax.broadcasted_iota(jnp.int32, (cap, xc), 1).astype(jnp.float32), 1.0, 0.0
            )
            mask_y[j] = jnp.where(
                jnp.broadcast_to(layer, (cap, nk)) == lax.broadcasted_iota(jnp.int32, (cap, nk), 1).astype(jnp.float32), 1.0, 0.0
            )
            return c

        lax.fori_loop(0, nn, body, 0)

    def prepare_owners():
        s_line = slot_line[...]
        base = ((lax.broadcasted_iota(jnp.int32, (nw, terms), 0) * nn + ni) * owned).astype(jnp.float32)
        s_all = jnp.broadcast_to(s_line, (nw, terms))
        owner_hot[...] = jnp.where((s_all >= base) & (s_all < base + owned), 1.0, 0.0)
        rest = s_line - owned * jnp.floor((s_line + 0.5) * (1.0 / owned))
        place_hot[...] = jnp.where(
            jnp.broadcast_to(rest, (nk, terms)) == lax.broadcasted_iota(jnp.int32, (nk, terms), 0).astype(jnp.float32), 1.0, 0.0
        )

    def cells_y():
        t_in = tin_r[:, 0, :]
        there = t_in > 0.0
        e0 = jnp.where(there, re_r[0, :, 0, :] * re_r[3, :, 0, :] / jnp.where(there, t_in, 1.0), 0.0)

        def body(j, before):
            e = ty_y[j] * (late1_y[j] - late1_y[j + 1]) * (p2_y[j] - p2_y[j + 1])
            c_y[j] = -0.5 * (e + before)
            return e

        before = lax.fori_loop(0, last, body, e0)

        def out_flux(rhs, v):
            return rhs[last] - st_y[last] * v[last] - ty_y[last - 1] * (v[last] - v[last - 1])

        e = jnp.where(wi == nw - 1, 0.0, out_flux(seed_y, late1_y) * out_flux(b1_y, p2_y) / ty_y[last])
        c_y[last] = -0.5 * (e + before)

    def pick_y():
        for j in range(nn):
            picked_y[j * cap : (j + 1) * cap, :] = mask_y[j] * jnp.dot(
                hot_y[j], c_y[j], precision=HIGHEST, preferred_element_type=jnp.float32
            )
        return lanes_to_line(picked_y[...])

    def start_y(rhs, number, slot, out):
        arrived(number, rhs)
        reduce_y(rhs, slot)
        spread_wide(T_S0 + slot, to_s.at[slot], to_r.at[slot])
        inside_y(rhs, out)

    def middle_y(slot):
        arrived(T_S0 + slot, to_r.at[slot])
        solve_sep(slot)
        spread_wide(T_R0 + slot, re_s.at[slot], re_r.at[slot])

    def end_y(slot, out, number=None, to_ref=None):
        arrived(T_R0 + slot, re_r.at[slot])
        complete_y(out, slot)
        if number is not None:
            to_x(number, out, to_ref)

    loads[0].wait()
    loads[1].wait()
    tx[PAD + nx - 1 : PAD + nx, :] = jnp.zeros((1, nk), jnp.float32)
    factor_x()
    for one in loads[2:]:
        one.wait()
    lane = lax.broadcasted_iota(jnp.int32, (bl, nk), 1)
    open_y = row < rows - 1

    arrived(T_TY, ty_y)
    arrived(T_ST, st_y)
    factor_y()
    spread_wide(T_COEF, coef_s, coef_r)

    for i in range(PIECES):
        rows_at = pl.ds(i * piece, piece)
        arrived(T_PIECE + i, part(p_next, i))
        tz[rows_at, :] = jnp.where(lane[0:piece] < nk - 1, tz[rows_at, :], 0.0)
        t = jnp.where(open_y, ty[rows_at, :], 0.0)
        ty[rows_at, :] = t
        flux[rows_at, :] = t * (p0[rows_at, :] - p_next[rows_at, :])
        remote(part(flux, i), part(f_prev, i), T_PIECE + PIECES + i, next_dev).start()

    start_y(seed_y, T_SEED, 0, late1_y)

    for i in range(PIECES):
        arrived(T_PIECE + PIECES + i, part(f_prev, i))

    def rhs_u0(o):
        ba[pl.ds(o + pad_x, bl), :] = at(src, o) - (at(flux, o) - at(f_prev, o)) - div_z(at(p0, o), o)

    each_block(rhs_u0)
    solve_x(u0)

    def make_b0(o):
        b0[pl.ds(o, bl), :] = at(src, o) - div_x(u0, o) - div_z(up(u0, o), o)

    each_block(make_b0)
    to_y(T_B0, b0, b0_y)

    arrived(T_COEF, coef_r)
    factor_sep()
    middle_y(0)

    start_y(b0_y, T_B0, 1, p1_y)
    arrived(T_CELL_P, cell_r.at[1])
    arrived(T_CELL_N, cell_r.at[0])
    prepare_picks()
    end_y(0, late1_y, T_LATE1, late1)
    middle_y(1)

    arrived(T_LATE1, inner(late1))

    def rhs_early(ref):
        def body(o):
            ba[pl.ds(o + pad_x, bl), :] = -(div_x(ref, o) + div_z(up(ref, o), o))

        each_block(body)

    rhs_early(late1)
    solve_x(early1)

    def make_rw(o):
        v = up(early1, o)
        rw[pl.ds(o, bl), :] = at(st, o) * v - div_z(v, o)

    each_block(make_rw)
    to_y(T_RW, rw, rw_y)
    end_y(1, p1_y, T_P1, p1)
    spread_wide(T_TIN, tin_s, tin_r)

    start_y(rw_y, T_RW, 2, w_y)
    prepare_group()
    prepare_owners()

    arrived(T_P1, inner(p1))

    def rhs_u1(o):
        v = up(p1, o)
        ba[pl.ds(o + pad_x, bl), :] = at(src, o) - at(b0, o) + at(st, o) * v - div_z(v, o)

    each_block(rhs_u1)
    solve_x(u1)

    def make_b1(o):
        b1[pl.ds(o, bl), :] = at(src, o) - div_x(u1, o) - div_z(up(u1, o), o)

    each_block(make_b1)
    to_y(T_B1, b1, b1_y)

    middle_y(2)
    pick_three(0)
    start_y(b1_y, T_B1, 3, p2_y)
    end_y(2, w_y, T_W, w_x)

    arrived(T_W, inner(w_x))

    def make_late0(o):
        late0[pl.ds(o + PAD, bl), :] = up(w_x, o) - up(early1, o)

    each_block(make_late0)
    rhs_early(late0)
    solve_x(early0)
    middle_y(3)

    def make_sums(o):
        sum0[pl.ds(o + PAD, bl), :] = up(late0, o) + up(early0, o)
        both = up(late1, o) + up(early1, o)
        sum1[pl.ds(o + PAD, bl), :] = both
        grad_out[pl.ds(o, bl), :] = up(w_x, o) + up(early0, o) + up(late1, o)

    each_block(make_sums)

    def face_x(o):
        a = (up(sum0, o) - up(sum0, o, 1)) * (up(u0, o) - up(u0, o, 1))
        b = (up(sum1, o) - up(sum1, o, 1)) * (up(u1, o) - up(u1, o, 1))
        ba[pl.ds(o + pad_x, bl), :] = up(tx, o) * (a + b)

    each_block(face_x)

    def step_z(v):
        return v - next_layer(v)

    def cells_xz(o):
        z = step_z(up(early0, o)) * step_z(at(p0, o)) + step_z(up(late0, o)) * step_z(up(u0, o))
        z = z + step_z(up(early1, o)) * step_z(up(p1, o)) + step_z(up(late1, o)) * step_z(up(u1, o))
        z = at(tz, o) * z
        fields[5, pl.ds(o + PAD, bl), :] = -0.5 * (big(ba, o) + big(ba, o, -1)) - 0.5 * (z + prev_layer(z))

    each_block(cells_xz)
    pick_three(3)
    remote(msg_p, msg_r.at[1], T_MSG_P, prev_dev).start()
    remote(msg_n, msg_r.at[0], T_MSG_N, next_dev).start()
    arrived(T_TIN, tin_r)

    end_y(3, p2_y)
    cells_y()
    from_block = pick_y()

    arrived(T_MSG_P, msg_r.at[1])
    arrived(T_MSG_N, msg_r.at[0])
    before = msg_r[0] - own_v[...]
    after = own_v[...] - msg_r[1]

    def pairs(d):
        return d[3:4] * d[0:1] + d[4:5] * d[1:2]

    own_line = own_v[5:6, :] - 0.5 * (own_v[2:3, :] * pairs(after) + msg_r[0, 2:3, :] * pairs(before))
    here = lax.broadcasted_iota(jnp.int32, (1, terms), 1) // cap == ni
    val_s[0] = from_block + jnp.where(here, jnp.concatenate([own_line[:, 0:cap]] * nn, axis=1), 0.0)
    spread_narrow(T_VAL, lambda j: val_s.at[0], val_r.at[ni])
    arrived(T_VAL, val_r)

    totals = jnp.sum(val_r[...], axis=0)
    part_s[:, 0, :] = lax.dot_general(
        owner_hot[...] * jnp.broadcast_to(totals, (nw, terms)), place_hot[...],
        (((1,), (1,)), ((), ())), precision=HIGHEST, preferred_element_type=jnp.float32,
    )
    spread_wide(T_PART, part_s, part_r)
    arrived(T_PART, part_r)
    well_out[...] = jnp.sum(part_r[...], axis=0)

    for number in (T_TY, T_ST, T_SEED, T_B0, T_RW, T_B1, T_LATE1, T_P1, T_W):
        sent(number, ty_y.at[pl.ds(0, nn - 1)])
    for i in range(PIECES):
        sent(T_PIECE + i, part(p_next, i))
        sent(T_PIECE + PIECES + i, part(flux, i))
    sent(T_CELL_P, cell_s)
    sent(T_CELL_N, cell_s)
    sent(T_MSG_P, msg_p)
    sent(T_MSG_N, msg_n)
    sent(T_SLOT, slot_r.at[pl.ds(0, nn - 1)])
    sent(T_VAL, val_r.at[pl.ds(0, nn - 1)])
    sent(T_TIN, tin_s.at[pl.ds(0, nw - 1)])
    sent(T_COEF, coef_s.at[pl.ds(0, nw - 1)])
    for slot in range(4):
        sent(T_S0 + slot, to_s.at[slot, pl.ds(0, nw - 1)])
        sent(T_R0 + slot, re_s.at[slot, pl.ds(0, nw - 1)])
    sent(T_PART, part_s.at[pl.ds(0, nw - 1)])


def local(
    source, pressure_start, trans_x, trans_y, trans_z, storage, adjoint_seed,
    comp_cell, comp_well, comp_count, well_slot,
):
    _, nx, nk = source.shape
    nw, nn = lax.axis_size("wide"), lax.axis_size("narrow")
    cap = comp_cell.shape[1]
    owned = well_slot.shape[0] // (nw * nn)
    xc = nx // nn
    pad_w = max(PAD, nw // 2)
    f32 = jnp.float32

    def plain():
        return pltpu.VMEM((nx, nk), f32)

    def padded():
        return pltpu.VMEM((nx + 2 * PAD, nk), f32)

    def wide_pad():
        return pltpu.VMEM((2 * nx, nk), f32)

    def block():
        return pltpu.VMEM((nn, xc, nk), f32)

    def sep_pad():
        return pltpu.VMEM((nw + 2 * pad_w, nk), f32)

    def sep():
        return pltpu.VMEM((nw, nk), f32)

    def many(make, number):
        return [make() for _ in range(number)]

    scratch = (
        [plain(), padded()] + many(plain, 5)
        + many(block, 6) + many(block, 8)
        + many(padded, 1) + many(plain, 3) + many(padded, 6)
        + [pltpu.VMEM((levels_of(nx), nx, nk), f32)] * 2 + many(plain, 2) + many(wide_pad, 3)
        + [pltpu.VMEM((nw, 4, nk), f32)] * 2 + [pltpu.VMEM((4, nw, 2, nk), f32)] * 4
        + many(sep_pad, 3) + [pltpu.VMEM((levels_of(nw), nw, nk), f32)] * 2 + many(sep, 4)
        + [pltpu.VMEM((1, nk), f32), pltpu.VMEM((2, 1, nk), f32), pltpu.VMEM((8, nk), f32)]
        + [pltpu.VMEM((3 * cap, nx), f32), pltpu.VMEM((3 * cap, nk), f32), pltpu.VMEM((3 * cap, nk), f32)]
        + [pltpu.VMEM((8, nk), f32)] * 3 + [pltpu.VMEM((2, 8, nk), f32)]
        + [pltpu.VMEM((1, 2, nk), f32), pltpu.VMEM((nn, 2, nk), f32)]
        + [pltpu.VMEM((1, 1, nn * cap), f32), pltpu.VMEM((nn, 1, nn * cap), f32)]
        + [pltpu.VMEM((nw, 1, nk), f32)] * 4
        + [block(), pltpu.VMEM((nn, cap, xc), f32), pltpu.VMEM((nn, cap, nk), f32), pltpu.VMEM((nn * cap, nk), f32)]
        + [pltpu.VMEM((1, nn * cap), f32), pltpu.VMEM((nw, nn * cap), f32), pltpu.VMEM((nk, nn * cap), f32)]
        + [pltpu.VMEM((6, nx + 2 * PAD, nk), f32)]
        + [pltpu.SemaphoreType.DMA((T_COUNT,)), pltpu.SemaphoreType.DMA((T_COUNT,)), pltpu.SemaphoreType.DMA((L_COUNT,))]
    )
    hbm = pl.BlockSpec(memory_space=pl.ANY)
    vmem = pl.BlockSpec(memory_space=pltpu.VMEM)
    smem = pl.BlockSpec(memory_space=pltpu.SMEM)
    grad, sums = pl.pallas_call(
        functools.partial(kernel, nw, nn, nx, nk, cap, owned),
        out_shape=(jax.ShapeDtypeStruct((nx, nk), f32), jax.ShapeDtypeStruct((1, nk), f32)),
        in_specs=[hbm] * 7 + [vmem, vmem, smem, vmem],
        out_specs=(vmem, vmem),
        scratch_shapes=scratch,
        compiler_params=pltpu.CompilerParams(
            collective_id=0, has_side_effects=True, vmem_limit_bytes=62 * 1024 * 1024
        ),
    )(
        source[0], pressure_start[0], trans_x[0], trans_y[0], trans_z[0], storage[0], adjoint_seed[0],
        comp_cell, comp_well, comp_count.reshape(1, 1), well_slot.reshape(-1, nk),
    )
    return grad[None], sums[0, :owned]


def solution(mesh):
    cells = P(("wide", "narrow"), None, None)
    placed = (cells,) * 7 + (P(("wide", "narrow"), None), P(("wide", "narrow"), None), P(("wide", "narrow")), P())
    return jax.shard_map(
        local, mesh=mesh, in_specs=placed, out_specs=(cells, P(("wide", "narrow"))), check_vma=False
    )
```

```python
import functools

import jax
import jax.numpy as jnp
from jax import lax
from jax.experimental import pallas as pl
from jax.experimental.pallas import tpu as pltpu
from jax.sharding import PartitionSpec as P

MESH = pl.DeviceIdType.MESH
HIGHEST = lax.Precision.HIGHEST
PAD = 8

(
    T_TY, T_ST, T_SEED, T_B0, T_RW, T_B1, T_LATE1, T_P1, T_W, T_TIN,
    T_PNEXT, T_FLUX, T_CELL_P, T_CELL_N, T_SLOT, T_VAL, T_MSG_P, T_MSG_N,
    T_COEF, T_S0, T_S1, T_S2, T_S3, T_R0, T_R1, T_R2, T_R3, T_PART, T_PIECE, T_COUNT_BASE,
) = range(30)
PIECES = 4
T_COUNT = T_PIECE + 2 * PIECES
L_SRC, L_P0, L_TX, L_TY, L_TZ, L_ST, L_COUNT = range(7)


def levels_of(extent):
    return max(1, (extent - 1).bit_length())


def kernel(
    nw, nn, nx, nk, cap, owned,
    source, pressure, trans_x, trans_y, trans_z, storage, seed, cell, well, count, slots,
    grad_out, well_out,
    src, tx, tz, st, p_next, flux, f_prev,
    ty_y, st_y, seed_y, b0_y, rw_y, b1_y,
    inv_y, m_y, ga_y, gb_y, late1_y, p1_y, w_y, p2_y,
    late1, b0, b1, rw, u0, u1, early1, late0, sum0, sum1,
    gain_l, gain_r, inv_x, mid_x, ba, bb, bc,
    coef_s, coef_r, to_s, to_r, re_s, re_r,
    ia, ib, ic, pk_l, pk_r, pk_inv, tau, kap, f0s,
    cell_s, cell_r, pick_rows, onehot, lane_mask, gathered, own_v, msg_p, msg_n, msg_r,
    slot_s, slot_r, val_s, val_r, part_s, part_r,
    tin_s, tin_r, c_y, hot_y, mask_y, picked_y, slot_line, owner_hot, place_hot,
    fields, send_sem, recv_sem, load_sem,
):
    p0, ty = fields.at[0, pl.ds(PAD, nx)], fields.at[2, pl.ds(PAD, nx)]
    p1, early0, w_x = fields.at[1], fields.at[3], fields.at[4]
    wi, ni = lax.axis_index("wide"), lax.axis_index("narrow")
    rows = nw * nn
    row = wi * nn + ni
    nxt, prv = lax.rem(row + 1, rows), lax.rem(row + rows - 1, rows)
    next_dev = {"wide": nxt // nn, "narrow": lax.rem(nxt, nn)}
    prev_dev = {"wide": prv // nn, "narrow": lax.rem(prv, nn)}
    xc = nx // nn
    lev, pad_x = levels_of(nx), nx // 2
    lev_w, pad_w = levels_of(nw), max(PAD, nw // 2)
    bl = min(512, nx)
    blocks = nx // bl

    barrier = pltpu.get_barrier_semaphore()

    def greet_narrow(k, c):
        pl.semaphore_signal(barrier, inc=1, device_id={"narrow": lax.rem(ni + k, nn)}, device_id_type=MESH)
        return c

    def greet_wide(k, c):
        pl.semaphore_signal(barrier, inc=1, device_id={"wide": lax.rem(wi + k, nw)}, device_id_type=MESH)
        return c

    pl.semaphore_signal(barrier, inc=1, device_id=next_dev, device_id_type=MESH)
    pl.semaphore_signal(barrier, inc=1, device_id=prev_dev, device_id_type=MESH)
    lax.fori_loop(1, nn, greet_narrow, 0)
    lax.fori_loop(1, nw, greet_wide, 0)

    loads = [
        pltpu.make_async_copy(storage, st, load_sem.at[L_ST]),
        pltpu.make_async_copy(trans_x, tx.at[pl.ds(PAD, nx)], load_sem.at[L_TX]),
        pltpu.make_async_copy(trans_y, ty, load_sem.at[L_TY]),
        pltpu.make_async_copy(pressure, p0, load_sem.at[L_P0]),
        pltpu.make_async_copy(source, src, load_sem.at[L_SRC]),
        pltpu.make_async_copy(trans_z, tz, load_sem.at[L_TZ]),
    ]
    for one in loads:
        one.start()

    def remote(from_ref, to_ref, number, device):
        return pltpu.make_async_remote_copy(
            src_ref=from_ref, dst_ref=to_ref, send_sem=send_sem.at[number], recv_sem=recv_sem.at[number],
            device_id=device, device_id_type=MESH,
        )

    def spread_narrow(number, from_of, to_ref):
        def body(k, c):
            j = lax.rem(ni + k, nn)
            remote(from_of(j), to_ref, number, {"narrow": j}).start()
            return c

        lax.fori_loop(1, nn, body, 0)
        pltpu.make_async_copy(from_of(ni), to_ref, recv_sem.at[number]).start()

    def spread_wide(number, from_ref, to_ref):
        def body(k, c):
            j = lax.rem(wi + k, nw)
            remote(from_ref.at[j], to_ref.at[wi], number, {"wide": j}).start()
            return c

        lax.fori_loop(1, nw, body, 0)
        pltpu.make_async_copy(from_ref.at[wi], to_ref.at[wi], recv_sem.at[number]).start()

    def chunk(ref):
        return lambda j: ref.at[pl.ds(pl.multiple_of(j * xc, xc), xc)]

    def to_y(number, from_ref, to_ref):
        spread_narrow(number, chunk(from_ref), to_ref.at[ni])

    def to_x(number, from_ref, to_ref):
        spread_narrow(number, lambda j: from_ref.at[j], to_ref.at[pl.ds(pl.multiple_of(PAD + ni * xc, PAD), xc)])

    def arrived(number, ref):
        pltpu.make_async_copy(ref, ref, recv_sem.at[number]).wait()

    def sent(number, ref):
        pltpu.make_async_copy(ref, ref, send_sem.at[number]).wait()

    def inner(ref):
        return ref.at[pl.ds(PAD, nx)]

    zeros_pad = jnp.zeros((PAD, nk), jnp.float32)
    for ref in (tx, late1, p1, w_x, u0, u1, early1, early0, late0, sum0, sum1):
        ref[0:PAD, :] = zeros_pad
        ref[PAD + nx : 2 * PAD + nx, :] = zeros_pad
    zeros_x = jnp.zeros((pad_x, nk), jnp.float32)
    for ref in (ba, bb, bc):
        ref[0:pad_x, :] = zeros_x
        ref[pad_x + nx : 2 * pad_x + nx, :] = zeros_x
    zeros_w = jnp.zeros((pad_w, nk), jnp.float32)
    for ref in (ia, ib, ic):
        ref[0:pad_w, :] = zeros_w
        ref[pad_w + nw : 2 * pad_w + nw, :] = zeros_w
    for ref in (own_v, msg_p, msg_n):
        ref[...] = jnp.zeros_like(ref)

    cell_s[...] = jnp.zeros_like(cell_s)
    cell_s[0:1, 0:cap] = cell[...].astype(jnp.float32)

    def column(line):
        eye = lax.broadcasted_iota(jnp.int32, (cap, nk), 0) == lax.broadcasted_iota(jnp.int32, (cap, nk), 1)
        return jnp.sum(jnp.where(eye, jnp.broadcast_to(line, (cap, nk)), 0.0), axis=1, keepdims=True)

    def lanes_to_line(values):
        ones = jnp.ones((8, nk), jnp.float32)
        return lax.dot_general(
            ones, values, (((1,), (1,)), ((), ())), precision=HIGHEST, preferred_element_type=jnp.float32
        )[0:1, :]

    pick_rows[...] = jnp.zeros_like(pick_rows)
    pick_rows[0:1, 0:cap] = well[...].astype(jnp.float32)
    well_col = column(pick_rows[0:1, :])
    slot_rows = slots.shape[0]
    high = jnp.floor(well_col * (1.0 / nk))
    low = well_col - high * nk
    table_hot = jnp.where(
        jnp.broadcast_to(high, (cap, slot_rows)) == lax.broadcasted_iota(jnp.int32, (cap, slot_rows), 1).astype(jnp.float32),
        1.0, 0.0,
    )
    table = jnp.dot(table_hot, slots[...].astype(jnp.float32), precision=HIGHEST, preferred_element_type=jnp.float32)
    table = jnp.where(
        jnp.broadcast_to(low, (cap, nk)) == lax.broadcasted_iota(jnp.int32, (cap, nk), 1).astype(jnp.float32), table, 0.0
    )
    live = lax.broadcasted_iota(jnp.int32, (1, cap), 1) < count[0, 0]
    slot_s[...] = jnp.full_like(slot_s, -1.0)
    slot_s[0, 0:1, 0:cap] = jnp.where(live, lanes_to_line(table), -1.0)
    slot_s[0, 1:2, 0:cap] = cell_s[0:1, 0:cap]

    pl.semaphore_wait(barrier, nn - 1 + nw - 1 + 2)

    to_y(T_TY, trans_y, ty_y)
    to_y(T_ST, storage, st_y)
    piece = nx // PIECES

    def part(ref, i):
        return ref.at[pl.ds(i * piece, piece)]

    for i in range(PIECES):
        remote(part(pressure, i), part(p_next, i), T_PIECE + i, prev_dev).start()
    to_y(T_SEED, seed, seed_y)
    remote(cell_s, cell_r.at[1], T_CELL_P, prev_dev).start()
    remote(cell_s, cell_r.at[0], T_CELL_N, next_dev).start()
    spread_narrow(T_SLOT, lambda j: slot_s.at[0], slot_r.at[ni])

    def each_block(body):
        def step(i, c):
            body(pl.multiple_of(i * bl, bl))
            return c

        lax.fori_loop(0, blocks, step, 0)

    def at(ref, o, shift=0):
        return ref[pl.ds(o + shift, bl), :]

    def up(ref, o, shift=0):
        return ref[pl.ds(o + (PAD + shift), bl), :]

    def big(ref, o, shift=0):
        return ref[pl.ds(o + (pad_x + shift), bl), :]

    def next_layer(v):
        return pltpu.roll(v, nk - 1, 1)

    def prev_layer(v):
        return pltpu.roll(v, 1, 1)

    def div_z(v, o):
        f = at(tz, o) * (v - next_layer(v))
        return f - prev_layer(f)

    def div_x(ref, o):
        v = up(ref, o)
        return up(tx, o) * (v - up(ref, o, 1)) - up(tx, o, -1) * (up(ref, o, -1) - v)

    def solve_x(out):
        pair = (ba, bb)
        for level in range(lev):
            stride = 1 << level
            a, b = pair[level % 2], pair[1 - level % 2]

            def body(o):
                v = big(a, o)
                v = v + gain_l[level, pl.ds(o, bl), :] * big(a, o, -stride)
                v = v + gain_r[level, pl.ds(o, bl), :] * big(a, o, stride)
                if level == lev - 1:
                    out[pl.ds(o + PAD, bl), :] = v * at(inv_x, o)
                else:
                    b[pl.ds(o + pad_x, bl), :] = v

            each_block(body)

    def factor_x():
        def begin(o):
            t = up(tx, o)
            bb[pl.ds(o + pad_x, bl), :] = -t
            mid_x[pl.ds(o, bl), :] = at(st, o) + t + up(tx, o, -1)

        each_block(begin)
        pair = (bb, bc)
        for level in range(lev):
            stride = 1 << level
            a, b = pair[level % 2], pair[1 - level % 2]

            def invert(o):
                ba[pl.ds(o + pad_x, bl), :] = 1.0 / at(mid_x, o)

            def body(o):
                ua, ul = big(a, o), big(a, o, -stride)
                left = ul * big(ba, o, -stride)
                right = ua * big(ba, o, stride)
                gain_l[level, pl.ds(o, bl), :] = -left
                gain_r[level, pl.ds(o, bl), :] = -right
                b[pl.ds(o + pad_x, bl), :] = -right * big(a, o, stride)
                mid_x[pl.ds(o, bl), :] = at(mid_x, o) - left * ul - right * ua

            each_block(invert)
            each_block(body)

        def finish(o):
            inv_x[pl.ds(o, bl), :] = 1.0 / at(mid_x, o)

        each_block(finish)

    last = nn - 1

    def factor_y():
        def down(j, carry):
            delta, e = carry
            t = ty_y[j]
            iv = 1.0 / (delta + t)
            m = t * iv
            inv_y[j] = iv
            m_y[j] = m
            ga_y[j] = e
            return st_y[j + 1] + m * delta, m * e

        dee, kappa = lax.fori_loop(0, last, down, (st_y[0], jnp.ones((xc, nk), jnp.float32)))

        def back(i, carry):
            a, b = carry
            j = last - 1 - i
            m = m_y[j]
            a = inv_y[j] * ga_y[j] + m * a
            b = m * b
            ga_y[j] = a
            gb_y[j] = b
            return a, b

        corner, _ = lax.fori_loop(
            0, last, back, (jnp.zeros((xc, nk), jnp.float32), jnp.ones((xc, nk), jnp.float32))
        )
        t_last = jnp.where(wi == nw - 1, 0.0, ty_y[last])
        for number, value in enumerate((dee, kappa, corner, t_last)):
            coef_s[:, number, :] = value

    def reduce_y(rhs, slot):
        def body(j, carry):
            a, f = carry
            v = rhs[j]
            return a + gb_y[j] * v, f + ga_y[j] * v

        a, f = lax.fori_loop(0, last, body, (rhs[last], jnp.zeros((xc, nk), jnp.float32)), unroll=True)
        to_s[slot, :, 0, :] = a
        to_s[slot, :, 1, :] = f

    def inside_y(rhs, out):
        def down(j, c):
            out[j] = c
            return rhs[j + 1] + m_y[j] * c

        lax.fori_loop(0, last, down, rhs[0])

        def back(i, c):
            j = last - 1 - i
            c = inv_y[j] * out[j] + m_y[j] * c
            out[j] = c
            return c

        lax.fori_loop(0, last, back, jnp.zeros((xc, nk), jnp.float32))

    def complete_y(out, slot):
        phi = re_r[slot, :, 0, :]
        sep = re_r[slot, :, 1, :]

        def body(j, c):
            out[j] = out[j] + ga_y[j] * phi + gb_y[j] * sep
            return c

        lax.fori_loop(0, last, body, 0, unroll=True)
        out[last] = sep

    def mid(ref, shift=0):
        return ref[pad_w + shift : pad_w + shift + nw, :]

    def put(ref, value):
        ref[pad_w : pad_w + nw, :] = value

    def factor_sep():
        dee, kappa, corner, t_last = (coef_r[:, number, :] for number in range(4))
        put(ia, t_last)
        t_in = mid(ia, -1)
        tau_v = t_in / (1.0 + t_in * corner)
        tau[...] = tau_v
        kap[...] = kappa
        tin_s[:, 0, :] = t_in
        put(ia, tau_v)
        put(ib, tau_v * kappa)
        middle = dee + mid(ia, 1) + kappa * kappa * tau_v
        upper = -mid(ib, 1)
        for level in range(lev_w):
            stride = 1 << level
            put(ia, 1.0 / middle)
            put(ib, upper)
            lower = mid(ib, -stride)
            left = lower * mid(ia, -stride)
            right = upper * mid(ia, stride)
            pk_l[level] = -left
            pk_r[level] = -right
            middle = middle - left * lower - right * upper
            upper = -right * mid(ib, stride)
        pk_inv[...] = 1.0 / middle

    def solve_sep(slot):
        alpha = to_r[slot, :, 0, :]
        f0 = to_r[slot, :, 1, :]
        tf = tau[...] * f0
        put(ic, tf)
        v = alpha + mid(ic, 1) - kap[...] * tf
        for level in range(lev_w):
            stride = 1 << level
            ref = (ia, ib)[level % 2]
            put(ref, v)
            v = v + pk_l[level] * mid(ref, -stride) + pk_r[level] * mid(ref, stride)
        v = v * pk_inv[...]
        put(ic, v)
        re_s[slot, :, 0, :] = tau[...] * (mid(ic, -1) - f0 - kap[...] * v)
        re_s[slot, :, 1, :] = v

    def prepare_picks():
        for number, line in enumerate((cell_s[0:1, :], cell_r[0], cell_r[1])):
            col = column(line)
            x_of = jnp.floor(col * (1.0 / nk))
            layer = col - x_of * nk
            rows_at = pl.ds(number * cap, cap)
            onehot[rows_at, :] = jnp.where(
                jnp.broadcast_to(x_of, (cap, nx)) == lax.broadcasted_iota(jnp.int32, (cap, nx), 1).astype(jnp.float32), 1.0, 0.0
            )
            lane_mask[rows_at, :] = jnp.where(
                jnp.broadcast_to(layer, (cap, nk)) == lax.broadcasted_iota(jnp.int32, (cap, nk), 1).astype(jnp.float32), 1.0, 0.0
            )

    def pick_three(first):
        def body(i, c):
            number = first + i
            gathered[...] = lane_mask[...] * jnp.dot(
                onehot[...], fields[number, pl.ds(PAD, nx), :], precision=HIGHEST, preferred_element_type=jnp.float32
            )
            own_v[pl.ds(number, 1), 0:cap] = lanes_to_line(gathered[0:cap, :])
            msg_p[pl.ds(number, 1), 0:cap] = lanes_to_line(gathered[cap : 2 * cap, :])
            msg_n[pl.ds(number, 1), 0:cap] = lanes_to_line(gathered[2 * cap : 3 * cap, :])
            return c

        lax.fori_loop(0, 3, body, 0)

    terms = nn * cap

    def prepare_group():
        arrived(T_SLOT, slot_r)
        for j in range(nn):
            slot_line[0:1, j * cap : (j + 1) * cap] = slot_r[j, 0:1, 0:cap]

        def body(j, c):
            col = column(slot_r[j, 1:2, :])
            x_of = jnp.floor(col * (1.0 / nk))
            layer = col - x_of * nk
            x_of = x_of - (ni * xc).astype(jnp.float32)
            hot_y[j] = jnp.where(
                jnp.broadcast_to(x_of, (cap, xc)) == lax.broadcasted_iota(jnp.int32, (cap, xc), 1).astype(jnp.float32), 1.0, 0.0
            )
            mask_y[j] = jnp.where(
                jnp.broadcast_to(layer, (cap, nk)) == lax.broadcasted_iota(jnp.int32, (cap, nk), 1).astype(jnp.float32), 1.0, 0.0
            )
            return c

        lax.fori_loop(0, nn, body, 0)

    def prepare_owners():
        s_line = slot_line[...]
        base = ((lax.broadcasted_iota(jnp.int32, (nw, terms), 0) * nn + ni) * owned).astype(jnp.float32)
        s_all = jnp.broadcast_to(s_line, (nw, terms))
        owner_hot[...] = jnp.where((s_all >= base) & (s_all < base + owned), 1.0, 0.0)
        rest = s_line - owned * jnp.floor((s_line + 0.5) * (1.0 / owned))
        place_hot[...] = jnp.where(
            jnp.broadcast_to(rest, (nk, terms)) == lax.broadcasted_iota(jnp.int32, (nk, terms), 0).astype(jnp.float32), 1.0, 0.0
        )

    def cells_y():
        t_in = tin_r[:, 0, :]
        there = t_in > 0.0
        e0 = jnp.where(there, re_r[0, :, 0, :] * re_r[3, :, 0, :] / jnp.where(there, t_in, 1.0), 0.0)

        def body(j, before):
            e = ty_y[j] * (late1_y[j] - late1_y[j + 1]) * (p2_y[j] - p2_y[j + 1])
            c_y[j] = -0.5 * (e + before)
            return e

        before = lax.fori_loop(0, last, body, e0)

        def out_flux(rhs, v):
            return rhs[last] - st_y[last] * v[last] - ty_y[last - 1] * (v[last] - v[last - 1])

        e = jnp.where(wi == nw - 1, 0.0, out_flux(seed_y, late1_y) * out_flux(b1_y, p2_y) / ty_y[last])
        c_y[last] = -0.5 * (e + before)

    def pick_y():
        for j in range(nn):
            picked_y[j * cap : (j + 1) * cap, :] = mask_y[j] * jnp.dot(
                hot_y[j], c_y[j], precision=HIGHEST, preferred_element_type=jnp.float32
            )
        return lanes_to_line(picked_y[...])

    def start_y(rhs, number, slot, out):
        arrived(number, rhs)
        reduce_y(rhs, slot)
        spread_wide(T_S0 + slot, to_s.at[slot], to_r.at[slot])
        inside_y(rhs, out)

    def middle_y(slot):
        arrived(T_S0 + slot, to_r.at[slot])
        solve_sep(slot)
        spread_wide(T_R0 + slot, re_s.at[slot], re_r.at[slot])

    def end_y(slot, out, number=None, to_ref=None):
        arrived(T_R0 + slot, re_r.at[slot])
        complete_y(out, slot)
        if number is not None:
            to_x(number, out, to_ref)

    loads[0].wait()
    loads[1].wait()
    tx[PAD + nx - 1 : PAD + nx, :] = jnp.zeros((1, nk), jnp.float32)
    factor_x()
    for one in loads[2:]:
        one.wait()
    lane = lax.broadcasted_iota(jnp.int32, (bl, nk), 1)
    open_y = row < rows - 1

    arrived(T_TY, ty_y)
    arrived(T_ST, st_y)
    factor_y()
    spread_wide(T_COEF, coef_s, coef_r)

    for i in range(PIECES):
        rows_at = pl.ds(i * piece, piece)
        arrived(T_PIECE + i, part(p_next, i))
        tz[rows_at, :] = jnp.where(lane[0:piece] < nk - 1, tz[rows_at, :], 0.0)
        t = jnp.where(open_y, ty[rows_at, :], 0.0)
        ty[rows_at, :] = t
        flux[rows_at, :] = t * (p0[rows_at, :] - p_next[rows_at, :])
        remote(part(flux, i), part(f_prev, i), T_PIECE + PIECES + i, next_dev).start()

    start_y(seed_y, T_SEED, 0, late1_y)

    for i in range(PIECES):
        arrived(T_PIECE + PIECES + i, part(f_prev, i))

    def rhs_u0(o):
        ba[pl.ds(o + pad_x, bl), :] = at(src, o) - (at(flux, o) - at(f_prev, o)) - div_z(at(p0, o), o)

    each_block(rhs_u0)
    solve_x(u0)

    def make_b0(o):
        b0[pl.ds(o, bl), :] = at(src, o) - div_x(u0, o) - div_z(up(u0, o), o)

    each_block(make_b0)
    to_y(T_B0, b0, b0_y)

    arrived(T_COEF, coef_r)
    factor_sep()
    middle_y(0)

    start_y(b0_y, T_B0, 1, p1_y)
    arrived(T_CELL_P, cell_r.at[1])
    arrived(T_CELL_N, cell_r.at[0])
    prepare_picks()
    end_y(0, late1_y, T_LATE1, late1)
    middle_y(1)

    arrived(T_LATE1, inner(late1))

    def rhs_early(ref):
        def body(o):
            ba[pl.ds(o + pad_x, bl), :] = -(div_x(ref, o) + div_z(up(ref, o), o))

        each_block(body)

    rhs_early(late1)
    solve_x(early1)

    def make_rw(o):
        v = up(early1, o)
        rw[pl.ds(o, bl), :] = at(st, o) * v - div_z(v, o)

    each_block(make_rw)
    to_y(T_RW, rw, rw_y)
    end_y(1, p1_y, T_P1, p1)
    spread_wide(T_TIN, tin_s, tin_r)

    start_y(rw_y, T_RW, 2, w_y)

    arrived(T_P1, inner(p1))

    def rhs_u1(o):
        v = up(p1, o)
        ba[pl.ds(o + pad_x, bl), :] = at(src, o) - at(b0, o) + at(st, o) * v - div_z(v, o)

    each_block(rhs_u1)
    solve_x(u1)

    def make_b1(o):
        b1[pl.ds(o, bl), :] = at(src, o) - div_x(u1, o) - div_z(up(u1, o), o)

    each_block(make_b1)
    to_y(T_B1, b1, b1_y)

    middle_y(2)
    pick_three(0)
    start_y(b1_y, T_B1, 3, p2_y)
    end_y(2, w_y, T_W, w_x)
    prepare_group()
    prepare_owners()

    arrived(T_W, inner(w_x))

    def make_late0(o):
        late0[pl.ds(o + PAD, bl), :] = up(w_x, o) - up(early1, o)

    each_block(make_late0)
    rhs_early(late0)
    solve_x(early0)
    middle_y(3)

    def make_sums(o):
        sum0[pl.ds(o + PAD, bl), :] = up(late0, o) + up(early0, o)
        both = up(late1, o) + up(early1, o)
        sum1[pl.ds(o + PAD, bl), :] = both
        grad_out[pl.ds(o, bl), :] = up(w_x, o) + up(early0, o) + up(late1, o)

    each_block(make_sums)

    def face_x(o):
        a = (up(sum0, o) - up(sum0, o, 1)) * (up(u0, o) - up(u0, o, 1))
        b = (up(sum1, o) - up(sum1, o, 1)) * (up(u1, o) - up(u1, o, 1))
        ba[pl.ds(o + pad_x, bl), :] = up(tx, o) * (a + b)

    each_block(face_x)

    def step_z(v):
        return v - next_layer(v)

    def cells_xz(o):
        z = step_z(up(early0, o)) * step_z(at(p0, o)) + step_z(up(late0, o)) * step_z(up(u0, o))
        z = z + step_z(up(early1, o)) * step_z(up(p1, o)) + step_z(up(late1, o)) * step_z(up(u1, o))
        z = at(tz, o) * z
        fields[5, pl.ds(o + PAD, bl), :] = -0.5 * (big(ba, o) + big(ba, o, -1)) - 0.5 * (z + prev_layer(z))

    each_block(cells_xz)
    pick_three(3)
    remote(msg_p, msg_r.at[1], T_MSG_P, prev_dev).start()
    remote(msg_n, msg_r.at[0], T_MSG_N, next_dev).start()
    arrived(T_TIN, tin_r)

    end_y(3, p2_y)
    cells_y()
    from_block = pick_y()

    arrived(T_MSG_P, msg_r.at[1])
    arrived(T_MSG_N, msg_r.at[0])
    before = msg_r[0] - own_v[...]
    after = own_v[...] - msg_r[1]

    def pairs(d):
        return d[3:4] * d[0:1] + d[4:5] * d[1:2]

    own_line = own_v[5:6, :] - 0.5 * (own_v[2:3, :] * pairs(after) + msg_r[0, 2:3, :] * pairs(before))
    here = lax.broadcasted_iota(jnp.int32, (1, terms), 1) // cap == ni
    val_s[0] = from_block + jnp.where(here, jnp.concatenate([own_line[:, 0:cap]] * nn, axis=1), 0.0)
    spread_narrow(T_VAL, lambda j: val_s.at[0], val_r.at[ni])
    arrived(T_VAL, val_r)

    totals = jnp.sum(val_r[...], axis=0)
    part_s[:, 0, :] = lax.dot_general(
        owner_hot[...] * jnp.broadcast_to(totals, (nw, terms)), place_hot[...],
        (((1,), (1,)), ((), ())), precision=HIGHEST, preferred_element_type=jnp.float32,
    )
    spread_wide(T_PART, part_s, part_r)
    arrived(T_PART, part_r)
    well_out[...] = jnp.sum(part_r[...], axis=0)

    for number in (T_TY, T_ST, T_SEED, T_B0, T_RW, T_B1, T_LATE1, T_P1, T_W):
        sent(number, ty_y.at[pl.ds(0, nn - 1)])
    for i in range(PIECES):
        sent(T_PIECE + i, part(p_next, i))
        sent(T_PIECE + PIECES + i, part(flux, i))
    sent(T_CELL_P, cell_s)
    sent(T_CELL_N, cell_s)
    sent(T_MSG_P, msg_p)
    sent(T_MSG_N, msg_n)
    sent(T_SLOT, slot_r.at[pl.ds(0, nn - 1)])
    sent(T_VAL, val_r.at[pl.ds(0, nn - 1)])
    sent(T_TIN, tin_s.at[pl.ds(0, nw - 1)])
    sent(T_COEF, coef_s.at[pl.ds(0, nw - 1)])
    for slot in range(4):
        sent(T_S0 + slot, to_s.at[slot, pl.ds(0, nw - 1)])
        sent(T_R0 + slot, re_s.at[slot, pl.ds(0, nw - 1)])
    sent(T_PART, part_s.at[pl.ds(0, nw - 1)])


def local(
    source, pressure_start, trans_x, trans_y, trans_z, storage, adjoint_seed,
    comp_cell, comp_well, comp_count, well_slot,
):
    _, nx, nk = source.shape
    nw, nn = lax.axis_size("wide"), lax.axis_size("narrow")
    cap = comp_cell.shape[1]
    owned = well_slot.shape[0] // (nw * nn)
    xc = nx // nn
    pad_w = max(PAD, nw // 2)
    f32 = jnp.float32

    def plain():
        return pltpu.VMEM((nx, nk), f32)

    def padded():
        return pltpu.VMEM((nx + 2 * PAD, nk), f32)

    def wide_pad():
        return pltpu.VMEM((2 * nx, nk), f32)

    def block():
        return pltpu.VMEM((nn, xc, nk), f32)

    def sep_pad():
        return pltpu.VMEM((nw + 2 * pad_w, nk), f32)

    def sep():
        return pltpu.VMEM((nw, nk), f32)

    def many(make, number):
        return [make() for _ in range(number)]

    scratch = (
        [plain(), padded()] + many(plain, 5)
        + many(block, 6) + many(block, 8)
        + many(padded, 1) + many(plain, 3) + many(padded, 6)
        + [pltpu.VMEM((levels_of(nx), nx, nk), f32)] * 2 + many(plain, 2) + many(wide_pad, 3)
        + [pltpu.VMEM((nw, 4, nk), f32)] * 2 + [pltpu.VMEM((4, nw, 2, nk), f32)] * 4
        + many(sep_pad, 3) + [pltpu.VMEM((levels_of(nw), nw, nk), f32)] * 2 + many(sep, 4)
        + [pltpu.VMEM((1, nk), f32), pltpu.VMEM((2, 1, nk), f32), pltpu.VMEM((8, nk), f32)]
        + [pltpu.VMEM((3 * cap, nx), f32), pltpu.VMEM((3 * cap, nk), f32), pltpu.VMEM((3 * cap, nk), f32)]
        + [pltpu.VMEM((8, nk), f32)] * 3 + [pltpu.VMEM((2, 8, nk), f32)]
        + [pltpu.VMEM((1, 2, nk), f32), pltpu.VMEM((nn, 2, nk), f32)]
        + [pltpu.VMEM((1, 1, nn * cap), f32), pltpu.VMEM((nn, 1, nn * cap), f32)]
        + [pltpu.VMEM((nw, 1, nk), f32)] * 4
        + [block(), pltpu.VMEM((nn, cap, xc), f32), pltpu.VMEM((nn, cap, nk), f32), pltpu.VMEM((nn * cap, nk), f32)]
        + [pltpu.VMEM((1, nn * cap), f32), pltpu.VMEM((nw, nn * cap), f32), pltpu.VMEM((nk, nn * cap), f32)]
        + [pltpu.VMEM((6, nx + 2 * PAD, nk), f32)]
        + [pltpu.SemaphoreType.DMA((T_COUNT,)), pltpu.SemaphoreType.DMA((T_COUNT,)), pltpu.SemaphoreType.DMA((L_COUNT,))]
    )
    hbm = pl.BlockSpec(memory_space=pl.ANY)
    vmem = pl.BlockSpec(memory_space=pltpu.VMEM)
    smem = pl.BlockSpec(memory_space=pltpu.SMEM)
    grad, sums = pl.pallas_call(
        functools.partial(kernel, nw, nn, nx, nk, cap, owned),
        out_shape=(jax.ShapeDtypeStruct((nx, nk), f32), jax.ShapeDtypeStruct((1, nk), f32)),
        in_specs=[hbm] * 7 + [vmem, vmem, smem, vmem],
        out_specs=(vmem, vmem),
        scratch_shapes=scratch,
        compiler_params=pltpu.CompilerParams(
            collective_id=0, has_side_effects=True, vmem_limit_bytes=62 * 1024 * 1024
        ),
    )(
        source[0], pressure_start[0], trans_x[0], trans_y[0], trans_z[0], storage[0], adjoint_seed[0],
        comp_cell, comp_well, comp_count.reshape(1, 1), well_slot.reshape(-1, nk),
    )
    return grad[None], sums[0, :owned]


def solution(mesh):
    cells = P(("wide", "narrow"), None, None)
    placed = (cells,) * 7 + (P(("wide", "narrow"), None), P(("wide", "narrow"), None), P(("wide", "narrow")), P())
    return jax.shard_map(
        local, mesh=mesh, in_specs=placed, out_specs=(cells, P(("wide", "narrow"))), check_vma=False
    )
```
